512 devices in a mesh: ep: 32 (over z, x), etp: 16 (over y, core).
Axes of the slice: x: 4, y: 8, z: 8, core: 2. Of those that a mesh axis runs over, the one named last changes fastest.
Arguments:
- tokens: bfloat16 [8192, 2560], P('ep', 'etp'), may hold values from -6 to 6
- grad_out: bfloat16 [8192, 2560], P('ep', 'etp'), may hold values from -6 to 6
- expert_ids: int32 [8192, 1], P('ep'), may hold values from 0 to 31; in each aligned block of 256 rows (0 to 255, 256 to 511, ...) at most 12 rows name the same one
- router: bfloat16 [2560, 32], P('etp'), may hold values from -0.078125 to 0.078125
- gate_weight: bfloat16 [32, 2560, 4096], P('ep', None, 'etp'), may hold values from -0.125 to 0.125
- up_weight: bfloat16 [32, 2560, 4096], P('ep', None, 'etp'), may hold values from -0.125 to 0.125
- down_weight: bfloat16 [32, 4096, 2560], P('ep', 'etp'), may hold values from -0.09375 to 0.09375
Outputs:
- d_tokens: bfloat16 [8192, 2560], P('ep', 'etp')
The draws below stay inside these ranges and needn't reach their ends.
Inputs may be any that keep to these rules, and one draw needn't show every extreme that they name: `expert_ids`: within the 256 tokens of one index of ep (aligned blocks of tokens), no expert is chosen by more than 12 tokens; every expert is chosen by some token.
All inputs are finite; a program needn't handle non-finite values.
Results may differ from the reference program's by a relative error of at most 0.012.
Values may be sent and summed in bfloat16 or wider, within the bound.
No kernel may reach another device: no remote copies, remote signals or barrier semaphores. Data moves between devices by JAX's collectives and lax.ppermute only.
A program may use at most 128 MiB of HBM per device.

```python
import math
import jax
import jax.numpy as jnp
import numpy as np
from jax import lax

D = 2560
FF = 4096
TOK_EP = 256
EXPERTS = 32
CAP = 12
TOKENS = 8192
N_EP = 32


def level_of(stream_key, extent, shards, least, top_value):
    def one(axis_at, parts):
        draws = jax.random.uniform(jax.random.fold_in(jax.random.fold_in(stream_key, 6), axis_at), (parts,), jnp.float32, least / len(shards), top_value / len(shards))
        return jnp.repeat(jnp.exp(draws), extent[axis_at] // parts).reshape((-1,) + (1,) * (len(extent) - axis_at - 1))

    level = one(*shards[0])
    for cut in shards[1:]:
        level = level * one(*cut)
    return level


def shared_out(own_key, own, number, rows, count, top, reach, slope):
    ranking = jax.random.permutation(own_key, count)
    heavy_load, ordinary = portions_of(count, rows * top, reach, slope, True), portions_of(count, rows * top, reach, slope, False)
    places = jnp.arange(count)

    def named(lengths, rotation):
        used = int((lengths > 0).sum())
        fixed = max(1, used // 4)
        passed = fixed + (places - fixed + rotation * (used - fixed)) % max(1, count - fixed)
        return jnp.zeros((count,), jnp.int32).at[ranking[jnp.where(places < fixed, places, passed)]].set(jnp.asarray(lengths, jnp.int32))

    lengths = jnp.where(number % 4 == 0, named(heavy_load, number // 4), named(ordinary, number - number // 4 - 1))
    mixed = jax.random.permutation(jax.random.fold_in(own, 3), count)
    giver, sink = mixed[0:count // 2 * 2:2], mixed[1:count // 2 * 2:2]
    slack = jnp.minimum(lengths[giver] - 1, reach - lengths[sink]) // 2
    slack = jnp.where((giver == ranking[0]) | (sink == ranking[0]) | (lengths[sink] == 0), 0, jnp.maximum(slack, 0))
    passed = jax.random.randint(jax.random.fold_in(own, 4), (count // 2,), 0, 1 << 20) % (slack + 1)
    lengths = lengths.at[giver].add(-passed).at[sink].add(passed)
    labels = jnp.searchsorted(jnp.cumsum(lengths), jnp.arange(rows * top), side="right").astype(jnp.int32)
    grid = labels.reshape(top, rows).T
    grid = grid[jax.random.permutation(jax.random.fold_in(own, 1), rows)]
    rotation = jax.random.randint(jax.random.fold_in(own, 2), (rows, 1), 0, top)
    return jnp.take_along_axis(grid, (jnp.arange(top)[None, :] + rotation) % top, axis=1)


def portions_of(number_of, total, most, slope, full):
    weights = [(1 << 20) // math.isqrt(rank ** slope) + 1 for rank in range(1, number_of + 1)]
    largest = most if full else min(most, max(-(-total // number_of), total * weights[0] // sum(weights)))
    least = 1 if total - largest >= number_of - 1 else 0
    holding, spare = [largest] + [least] * (number_of - 1), total - largest - least * (number_of - 1)
    while spare > 0:
        free = [i for i in range(1, number_of) if holding[i] < largest] or [i for i in range(1, number_of) if holding[i] < most]
        whole, budget = sum([weights[i] for i in free]), spare
        for i in free:
            addition = min(most - holding[i], max(1, budget * weights[i] // whole), spare)
            holding[i] = holding[i] + addition
            spare = spare - addition
    return np.array(holding)


def normal_values(stream_key, shape, deviation, limit, cuts=(), kind=jnp.bfloat16):
    result = jax.random.normal(stream_key, shape, jnp.float32) * deviation
    if len(cuts) > 0:
        result = level_of(stream_key, shape, cuts, -0.22, 0.18) * result
    return jnp.clip(result, min=-limit, max=limit).astype(kind)


def setup_inputs(seed: int = 0) -> dict:
    key_of = jax.random.split(jax.random.key(seed), 8)
    tokens = normal_values(key_of[0], (TOKENS, D), 1.0, 6.0, ((0, 32), (1, 16)))
    grad_out = normal_values(key_of[1], (TOKENS, D), 1.0, 6.0, ((0, 32), (1, 16)))
    expert_ids_keys = jax.random.split(jax.random.fold_in(key_of[2], 1), TOKENS // TOK_EP)
    expert_ids_turns = jax.random.permutation(jax.random.fold_in(key_of[2], 3), TOKENS // TOK_EP)
    expert_ids = jax.vmap(lambda own, number: shared_out(jax.random.fold_in(key_of[2], 2), own, number, TOK_EP, EXPERTS, 1, CAP, 2))(expert_ids_keys, expert_ids_turns).reshape((TOKENS, 1))
    router = normal_values(key_of[3], (D, EXPERTS), (2 * D) ** -0.5, 0.078125, ((0, 16),))
    gate_weight = normal_values(key_of[4], (EXPERTS, D, FF), D ** -0.5, 0.125, ((0, 32), (2, 16)))
    up_weight = normal_values(key_of[5], (EXPERTS, D, FF), D ** -0.5, 0.125, ((0, 32), (2, 16)))
    down_weight = normal_values(key_of[6], (EXPERTS, FF, D), FF ** -0.5, 0.09375, ((0, 32), (1, 16)))
    return dict(tokens=tokens, grad_out=grad_out, expert_ids=expert_ids, router=router, gate_weight=gate_weight, up_weight=up_weight, down_weight=down_weight)


def silu_parts(gate_pre):
    sigmoid = jax.nn.sigmoid(gate_pre)
    return (gate_pre * sigmoid, sigmoid * (1.0 + gate_pre * (1.0 - sigmoid)))

def contract_last(left, right):
    return lax.dot_general(left, right, (((1,), (1,)), ((), ())), preferred_element_type=jnp.float32)

def input_grad(gate_pre, up_pre, d_hidden, w_gate, w_up):
    activated, slope_term = silu_parts(gate_pre)
    d_gate = (d_hidden * up_pre * slope_term).astype(jnp.bfloat16)
    d_up = (d_hidden * activated).astype(jnp.bfloat16)
    return contract_last(d_gate, w_gate) + contract_last(d_up, w_up)

def per_expert(items):
    flat_in, flat_grad, w_gate, w_up, w_down = items
    gate_pre = jnp.dot(flat_in, w_gate, preferred_element_type=jnp.float32)
    up_pre = jnp.dot(flat_in, w_up, preferred_element_type=jnp.float32)
    d_hidden = contract_last(flat_grad, w_down)
    return input_grad(gate_pre, up_pre, d_hidden, w_gate, w_up)

def reference(tokens, grad_out, expert_ids, router, gate_weight, up_weight, down_weight):
    chosen = expert_ids[:, 0].astype(jnp.int32)
    picked = chosen[:, None] == jnp.arange(EXPERTS, dtype=jnp.int32)[None, :]
    logits = jnp.dot(tokens, router, preferred_element_type=jnp.float32)
    logit_sum = lax.optimization_barrier(jnp.sum(jnp.where(picked, logits, 0.0), axis=1))
    scores = jax.nn.sigmoid(logit_sum)
    routed = (scores[:, None] * tokens.astype(jnp.float32)).astype(jnp.bfloat16)
    running = jnp.cumsum(picked.astype(jnp.int32), axis=0) - 1
    slot_rank = lax.optimization_barrier(jnp.sum(jnp.where(picked, running, 0), axis=1)).astype(jnp.int32)
    grid_rows = N_EP * CAP
    slot_index = (chosen * grid_rows + slot_rank).astype(jnp.int32)
    grid_in = jnp.zeros((EXPERTS * grid_rows, D), jnp.bfloat16).at[slot_index].set(routed)
    grid_grad = jnp.zeros((EXPERTS * grid_rows, D), jnp.bfloat16).at[slot_index].set(grad_out)
    grid_in = grid_in.reshape(EXPERTS, grid_rows, D)
    grid_grad = grid_grad.reshape(EXPERTS, grid_rows, D)
    back_grid = lax.map(per_expert, (grid_in, grid_grad, gate_weight, up_weight, down_weight))
    d_routed = back_grid.reshape(EXPERTS * grid_rows, D)[slot_index].astype(jnp.bfloat16)
    d_score = lax.optimization_barrier(jnp.sum(d_routed.astype(jnp.float32) * tokens.astype(jnp.float32), axis=1))
    d_logit = d_score * scores * (1.0 - scores)
    router_cols = contract_last(picked.astype(jnp.bfloat16), router)
    d_tokens = scores[:, None] * d_routed.astype(jnp.float32) + d_logit[:, None] * router_cols
    return d_tokens.astype(jnp.bfloat16)
```

```python
import jax
import jax.numpy as jnp
from jax import lax
from jax.experimental import pallas as pl
from jax.experimental.pallas import tpu as pltpu
from jax.sharding import PartitionSpec as P

CAP = 12
ROWS = 16
EXPERTS = 32
TOK = 256
WID = 160
N_ETP = 16
D = WID * N_ETP
HID = 256
SLOTS = EXPERTS * CAP
HALF = SLOTS // 2
GRID = EXPERTS * ROWS
AG_ROWS = 2 * WID + 16
F32 = jnp.float32
BF = jnp.bfloat16


def iota(shape, dim):
    return lax.broadcasted_iota(jnp.int32, shape, dim)


def dot(left, right, dims):
    return lax.dot_general(left, right, ((dims[:1], dims[1:]), ((), ())), preferred_element_type=F32)


def slot_lanes():
    row = iota((GRID, 1), 0)
    src, rank = row // ROWS, row % ROWS
    half = src // (EXPERTS // 2)
    at = (src % (EXPERTS // 2)) * CAP + rank
    lane = jnp.where(at < 128, half * 128 + at, 256 + half * 64 + at - 128)
    lane = jnp.where(rank < CAP, lane, -1)
    return (lane == iota((GRID, SLOTS), 1)).astype(BF)


def pack_kernel(ids_ref, x_ref, g_ref, send_ref, slot_ref):
    ids = ids_ref[...]
    picked = iota((EXPERTS, TOK), 0) == ids
    before = (iota((TOK, TOK), 0) < iota((TOK, TOK), 1)).astype(BF)
    earlier = dot(picked.astype(BF), before, (1, 0))
    rank = jnp.sum(jnp.where(picked, earlier, 0.0), axis=0, keepdims=True).astype(jnp.int32)
    slot = ids * ROWS + rank
    slot_ref[...] = slot
    place = (iota((GRID, TOK), 0) == slot).astype(BF)
    both = jnp.concatenate([x_ref[...], g_ref[...]], axis=0)
    send_ref[...] = dot(place, both, (1, 1)).astype(BF)


def turn_kernel(me_ref, recv_ref, router_ref, out_ref):
    out_ref[: 2 * WID, :] = dot(recv_ref[...], slot_lanes(), (0, 0)).astype(BF)
    mine = (iota((16, EXPERTS), 1) == me_ref[0]).astype(BF)
    column = dot(mine, router_ref[...], (1, 0)).astype(BF)
    out_ref[2 * WID :, :] = jnp.concatenate([column, jnp.zeros((16, SLOTS - WID), BF)], axis=1)


def expert_kernel(core_ref, ag_ref, wg0, wg1, wu0, wu1, wd0, wd1, out_ref, x_ref, g_ref, r_ref, wg, wu, wd, sems):
    lanes = pl.ds(pl.multiple_of(core_ref[0] * 128, 128), 128)
    rest = pl.ds(256, 128)

    def cp(src, dst, k):
        c = pltpu.make_async_copy(src, dst, sems.at[k])
        c.start()
        return c

    def blocks(first, dst, k):
        got = []
        for j in range(N_ETP):
            rows, to = pl.ds(first, WID), pl.ds(j * WID, WID)
            got.append(cp(ag_ref.at[j, rows, lanes], dst.at[to, pl.ds(0, 128)], k + 2 * j))
            got.append(cp(ag_ref.at[j, rows, rest], dst.at[to, pl.ds(128, 128)], k + 2 * j + 1))
        return got

    n = 2 * N_ETP
    get_r = [cp(ag_ref.at[j, pl.ds(2 * WID, 16), pl.ds(0, 256)], r_ref.at[pl.ds(16 * j, 16)], 2 * n + j) for j in range(N_ETP)]
    get_x = blocks(0, x_ref, 0)
    k = 2 * n + N_ETP
    get_wg = [cp(w, wg.at[h], k + h) for h, w in enumerate((wg0, wg1))]
    get_wu = [cp(w, wu.at[h], k + 2 + h) for h, w in enumerate((wu0, wu1))]
    get_g = blocks(WID, g_ref, n)
    get_wd = [cp(w, wd.at[h], k + 4 + h) for h, w in enumerate((wd0, wd1))]

    for c in get_r + get_x:
        c.wait()
    x = x_ref[...]
    router = r_ref[...].astype(F32).T
    logit = jnp.zeros((1, 256), F32)
    for j in range(N_ETP):
        logit += jnp.sum(x_ref[pl.ds(j * WID, WID), :].astype(F32) * router[:WID, 16 * j : 16 * j + 1], axis=0, keepdims=True)
    score = 1.0 / (1.0 + jnp.exp(-logit))
    for c in get_wg:
        c.wait()
    gate = [dot(x, wg[h], (0, 0)).T for h in range(2)]
    for c in get_wu:
        c.wait()
    up = [dot(x, wu[h], (0, 0)).T for h in range(2)]
    for c in get_g + get_wd:
        c.wait()
    g = g_ref[...]
    d_gate, d_up = [], []
    d_score = jnp.zeros((1, 256), F32)
    for h in range(2):
        d_hidden = dot(wd[h], g, (1, 0))
        gate_pre, up_pre = gate[h] * score, up[h] * score
        sig = 1.0 / (1.0 + jnp.exp(-gate_pre))
        dg = (d_hidden * up_pre * (sig * (1.0 + gate_pre * (1.0 - sig)))).astype(BF)
        du = (d_hidden * (gate_pre * sig)).astype(BF)
        d_score += jnp.sum(dg.astype(F32) * gate[h] + du.astype(F32) * up[h], axis=0, keepdims=True)
        d_gate.append(dg)
        d_up.append(du)
    d_logit = d_score * score * (1.0 - score)
    keep = (iota((WID // 2, 128), 1) // 64) == core_ref[0]
    for j in range(N_ETP):
        rows = pl.ds(j * WID, WID)
        total = dot(wg[0, rows, :], d_gate[0], (1, 0)) + dot(wg[1, rows, :], d_gate[1], (1, 0))
        total += dot(wu[0, rows, :], d_up[0], (1, 0)) + dot(wu[1, rows, :], d_up[1], (1, 0))
        total = total * score + router[:WID, 16 * j : 16 * j + 1] * d_logit
        out_ref[j, :WID, :] = total[:, :128].astype(BF)
        top, bottom = total[: WID // 2, 128:], total[WID // 2 :, 128:]
        out_ref[j, WID:, :] = jnp.where(keep, top, pltpu.roll(bottom, 64, 1)).astype(BF)


def sum_kernel(recv_ref, out_ref):
    parts = []
    for c in range(2):
        total = recv_ref[c].astype(F32)
        for y in range(1, N_ETP // 2):
            total += recv_ref[2 * y + c].astype(F32)
        parts.append(total)
    first = iota((WID // 2, 128), 1) < 64
    top = jnp.where(first, parts[0][WID:], parts[1][WID:])
    bottom = jnp.where(first, pltpu.roll(parts[0][WID:], 64, 1), pltpu.roll(parts[1][WID:], 64, 1))
    whole = jnp.concatenate([parts[0][:WID], parts[1][:WID], jnp.concatenate([top, bottom], axis=0)], axis=1)
    out_ref[...] = dot(slot_lanes(), whole.astype(BF), (1, 1)).astype(BF)


def unpack_kernel(slot_ref, recv_ref, out_ref):
    place = (iota((GRID, TOK), 0) == slot_ref[...]).astype(BF)
    out_ref[...] = dot(recv_ref[...], place, (0, 0)).astype(BF)


VM = pl.BlockSpec(memory_space=pltpu.VMEM)
SM = pl.BlockSpec(memory_space=pltpu.SMEM)
ANY = pl.BlockSpec(memory_space=pl.ANY)


def call(kernel, ins, outs, out_specs=VM, scratch=(), vmem=32 << 20, cost=None):
    return pl.pallas_call(
        kernel,
        out_shape=outs,
        in_specs=ins,
        out_specs=out_specs,
        scratch_shapes=list(scratch),
        cost_estimate=cost,
        compiler_params=pltpu.CompilerParams(vmem_limit_bytes=vmem),
    )


def body(tokens, grad_out, expert_ids, router, gate_weight, up_weight, down_weight):
    me = lax.axis_index("ep").astype(jnp.int32).reshape(1)
    core = (lax.axis_index("etp") % 2).astype(jnp.int32).reshape(1)
    other = [(i, i ^ 1) for i in range(N_ETP)]
    own = [gate_weight[0], up_weight[0], down_weight[0]]
    shape = jax.ShapeDtypeStruct

    send, slot = call(pack_kernel, [VM] * 3, [shape((GRID, 2 * WID), BF), shape((1, TOK), jnp.int32)], [VM] * 2)(
        expert_ids.reshape(1, TOK), tokens.T, grad_out.T
    )
    recv = lax.all_to_all(send.reshape(EXPERTS, ROWS, 2 * WID), "ep", split_axis=0, concat_axis=0, tiled=True)
    turned = call(turn_kernel, [SM, VM, VM], shape((AG_ROWS, SLOTS), BF))(me, recv.reshape(GRID, 2 * WID), router.T)
    gathered = lax.all_gather(turned, "etp", axis=0, tiled=True).reshape(N_ETP, AG_ROWS, SLOTS)
    wg, wu, wd = own
    wg1, wu1, wd1 = (lax.ppermute(w, "etp", other) for w in own)
    partial = call(
        expert_kernel,
        [SM] + [ANY] * 7,
        shape((N_ETP, WID * 3 // 2, 128), BF),
        scratch=[
            pltpu.VMEM((D, 256), BF),
            pltpu.VMEM((D, 256), BF),
            pltpu.VMEM((256, 256), BF),
            pltpu.VMEM((2, D, HID), BF),
            pltpu.VMEM((2, D, HID), BF),
            pltpu.VMEM((2, HID, D), BF),
            pltpu.SemaphoreType.DMA((4 * N_ETP + N_ETP + 6,)),
        ],
        vmem=48 << 20,
        cost=pl.CostEstimate(flops=10 * D * 512 * 256, bytes_accessed=12 << 20, transcendentals=512 * 256),
    )(core, gathered, wg, wg1, wu, wu1, wd, wd1)
    parts = lax.all_to_all(partial, "etp", split_axis=0, concat_axis=0, tiled=True)
    summed = call(sum_kernel, [VM], shape((GRID, WID), BF))(parts)
    back = lax.all_to_all(summed.reshape(EXPERTS, ROWS, WID), "ep", split_axis=0, concat_axis=0, tiled=True)
    out = call(unpack_kernel, [VM] * 2, shape((WID, TOK), BF))(slot, back.reshape(GRID, WID))
    return out.T


def solution(mesh):
    placed = (
        P("ep", "etp"),
        P("ep", "etp"),
        P("ep", None),
        P("etp", None),
        P("ep", None, "etp"),
        P("ep", None, "etp"),
        P("ep", "etp", None),
    )
    return jax.shard_map(body, mesh=mesh, in_specs=placed, out_specs=P("ep", "etp"), check_vma=False)
```

```python
import jax
import jax.numpy as jnp
from jax import lax
from jax.experimental import pallas as pl
from jax.experimental.pallas import tpu as pltpu
from jax.sharding import PartitionSpec as P

CAP = 12
ROWS = 16
EXPERTS = 32
TOK = 256
WID = 160
N_ETP = 16
D = WID * N_ETP
HID = 256
SLOTS = EXPERTS * CAP
HALF = SLOTS // 2
GRID = EXPERTS * ROWS
AG_ROWS = 2 * WID + 8
F32 = jnp.float32
BF = jnp.bfloat16


def iota(shape, dim):
    return lax.broadcasted_iota(jnp.int32, shape, dim)


def dot(left, right, dims):
    return lax.dot_general(left, right, ((dims[:1], dims[1:]), ((), ())), preferred_element_type=F32)


def slot_lanes():
    row = iota((GRID, 1), 0)
    src, rank = row // ROWS, row % ROWS
    half = src // (EXPERTS // 2)
    at = (src % (EXPERTS // 2)) * CAP + rank
    lane = jnp.where(at < 128, half * 128 + at, 256 + half * 64 + at - 128)
    lane = jnp.where(rank < CAP, lane, -1)
    return (lane == iota((GRID, SLOTS), 1)).astype(BF)


def power(k):
    size, out = jnp.abs(k).astype(jnp.int32), jnp.ones_like(k)
    for bit in range(7):
        factor = jnp.where(k < 0, 2.0 ** -(1 << bit), 2.0 ** (1 << bit))
        out = jnp.where((size & (1 << bit)) != 0, out * factor, out)
    return out


def level(top):
    return 14.0 - jnp.clip(jnp.floor(jnp.log2(jnp.maximum(top, 1e-36))), -110.0, 14.0)


def pack_kernel(ids_ref, x_ref, g_ref, send_ref, slot_ref, ids_v, x_v, g_v, sems):
    copies = [
        pltpu.make_async_copy(src, dst, sems.at[i])
        for i, (src, dst) in enumerate(((ids_ref, ids_v), (x_ref, x_v), (g_ref, g_v)))
    ]
    for c in copies:
        c.start()
    for c in copies:
        c.wait()
    ids = ids_v[...]
    picked = iota((EXPERTS, TOK), 0) == ids
    before = (iota((TOK, TOK), 0) < iota((TOK, TOK), 1)).astype(BF)
    earlier = dot(picked.astype(BF), before, (1, 0))
    rank = jnp.sum(jnp.where(picked, earlier, 0.0), axis=0, keepdims=True).astype(jnp.int32)
    slot = ids * ROWS + rank
    slot_ref[...] = slot
    place = (iota((GRID, TOK), 0) == slot).astype(BF)
    both = jnp.concatenate([x_v[...], g_v[...]], axis=0)
    send_ref[...] = dot(place, both, (1, 1)).astype(BF)


def router_kernel(me_ref, router_ref, out_ref):
    mine = (iota((8, EXPERTS), 1) == me_ref[0]).astype(BF)
    column = dot(mine, router_ref[...], (1, 0))
    shift = level(jnp.max(jnp.abs(column), axis=1, keepdims=True))
    scaled = column * power(shift)
    row = jnp.concatenate([scaled[:, :128], scaled[:, :128], scaled[:, 128:], jnp.zeros((8, 96), F32)], axis=1)
    out_ref[...] = jnp.where(iota((8, SLOTS), 0) == 0, row, jnp.broadcast_to(shift, (8, SLOTS)))


def turn_kernel(recv_ref, router_ref, out_ref):
    both = dot(recv_ref[...], slot_lanes(), (0, 0))
    shifts = []
    for i in range(2):
        half = both[i * WID : (i + 1) * WID]
        shift = level(jnp.max(jnp.abs(half), axis=0, keepdims=True))
        out_ref[i * WID : (i + 1) * WID, :] = half * power(shift)
        shifts.append(shift)
    row = iota((8, SLOTS), 0)
    out_ref[2 * WID :, :] = jnp.where(row < 2, router_ref[...], jnp.where(row == 2, shifts[0], shifts[1]))


def expert_kernel(core_ref, lo_ref, hi_ref, wg0, wu0, wd_other, wg_own, wu_own, wd_own, out_ref, x_ref, g_ref, wd0, wg1, wu1, wd1, sems):
    copies = [
        pltpu.make_async_copy(src, dst, sems.at[i])
        for i, (src, dst) in enumerate(((wd_other, wd0), (wg_own, wg1), (wu_own, wu1), (wd_own, wd1)))
    ]
    for c in copies:
        c.start()

    def rows(first, count):
        return jnp.concatenate([lo_ref[:, first : first + count, :], hi_ref[:, first : first + count, :]], axis=2)

    extra = rows(2 * WID, 8).astype(F32)
    back = power(-extra)
    logit = jnp.zeros((1, 256), F32)
    columns = []
    for j in range(N_ETP):
        at = pl.ds(j * WID, WID)
        for first, ref, row in ((0, x_ref, 2), (WID, g_ref, 3)):
            scale = back[j, row : row + 1, :].astype(BF)
            ref[at, :128] = lo_ref[j, first : first + WID, :] * scale[:, :128]
            ref[at, 128:] = hi_ref[j, first : first + WID, :] * scale[:, 128:]
        line = (extra[j, :8] * back[j, 1:2])[:, :WID]
        column = line.T[:, :1]
        logit += jnp.sum(x_ref[at, :].astype(F32) * column, axis=0, keepdims=True)
        columns.append(column)
    score = 1.0 / (1.0 + jnp.exp(-logit))
    xt = x_ref[...].T
    g = g_ref[...]
    d_gate, d_up = [], []
    d_score = jnp.zeros((1, 256), F32)
    for h, (wg, wu, wd) in enumerate(((wg0, wu0, wd0), (wg1, wu1, wd1))):
        for c in copies[1:] if h else copies[:1]:
            c.wait()
        gate = dot(xt, wg[...], (1, 0)).T
        up = dot(xt, wu[...], (1, 0)).T
        d_hidden = dot(wd[...], g, (1, 0))
        gate_pre, up_pre = gate * score, up * score
        sig = 1.0 / (1.0 + jnp.exp(-gate_pre))
        dg = (d_hidden * up_pre * (sig * (1.0 + gate_pre * (1.0 - sig)))).astype(BF)
        du = (d_hidden * (gate_pre * sig)).astype(BF)
        d_score += jnp.sum(dg.astype(F32) * gate + du.astype(F32) * up, axis=0, keepdims=True)
        d_gate.append(dg)
        d_up.append(du)
    d_logit = d_score * score * (1.0 - score)
    keep = (iota((WID // 2, 128), 1) // 64) == core_ref[0]
    for j in range(N_ETP):
        at = pl.ds(j * WID, WID)
        total = dot(wg0[at, :], d_gate[0], (1, 0)) + dot(wg1[at, :], d_gate[1], (1, 0))
        total += dot(wu0[at, :], d_up[0], (1, 0)) + dot(wu1[at, :], d_up[1], (1, 0))
        total = total * score + columns[j] * d_logit
        out_ref[j, :WID, :] = total[:, :128].astype(BF)
        top, bottom = total[: WID // 2, 128:], total[WID // 2 :, 128:]
        out_ref[j, WID:, :] = jnp.where(keep, top, pltpu.roll(bottom, 64, 1)).astype(BF)


def sum_kernel(recv_ref, out_ref):
    parts = []
    for c in range(2):
        total = recv_ref[c].astype(F32)
        for y in range(1, N_ETP // 2):
            total += recv_ref[2 * y + c].astype(F32)
        parts.append(total)
    first = iota((WID // 2, 128), 1) < 64
    top = jnp.where(first, parts[0][WID:], parts[1][WID:])
    bottom = jnp.where(first, pltpu.roll(parts[0][WID:], 64, 1), pltpu.roll(parts[1][WID:], 64, 1))
    whole = jnp.concatenate([parts[0][:WID], parts[1][:WID], jnp.concatenate([top, bottom], axis=0)], axis=1)
    out_ref[...] = dot(slot_lanes(), whole.astype(BF), (1, 1)).astype(BF)


def unpack_kernel(slot_ref, recv_ref, out_ref):
    place = (iota((GRID, TOK), 0) == slot_ref[...]).astype(BF)
    out_ref[...] = dot(recv_ref[...], place, (0, 0)).astype(BF)


VM = pl.BlockSpec(memory_space=pltpu.VMEM)
SM = pl.BlockSpec(memory_space=pltpu.SMEM)
HBM = pl.BlockSpec(memory_space=pltpu.HBM)


def in_hbm(x):
    return pltpu.with_memory_space_constraint(x, pltpu.HBM)


def call(kernel, ins, outs, out_specs=VM, scratch=(), vmem=32 << 20, cost=None):
    return pl.pallas_call(
        kernel,
        out_shape=outs,
        in_specs=ins,
        out_specs=out_specs,
        scratch_shapes=list(scratch),
        cost_estimate=cost,
        compiler_params=pltpu.CompilerParams(vmem_limit_bytes=vmem),
    )


def body(tokens, grad_out, expert_ids, router, gate_weight, up_weight, down_weight):
    me = lax.axis_index("ep").astype(jnp.int32).reshape(1)
    core = (lax.axis_index("etp") % 2).astype(jnp.int32).reshape(1)
    other = [(i, i ^ 1) for i in range(N_ETP)]
    own = [gate_weight[0], up_weight[0], down_weight[0]]
    shape = jax.ShapeDtypeStruct

    send, slot = call(
        pack_kernel,
        [HBM] * 3,
        [shape((GRID, 2 * WID), BF), shape((1, TOK), jnp.int32)],
        [VM] * 2,
        [pltpu.VMEM((1, TOK), jnp.int32), pltpu.VMEM((WID, TOK), BF), pltpu.VMEM((WID, TOK), BF), pltpu.SemaphoreType.DMA((3,))],
    )(in_hbm(expert_ids.reshape(1, TOK)), in_hbm(tokens.T), in_hbm(grad_out.T))
    line = call(router_kernel, [SM, VM], shape((8, SLOTS), F32))(me, router.T)
    recv = lax.all_to_all(send.reshape(EXPERTS, ROWS, 2 * WID), "ep", split_axis=0, concat_axis=0, tiled=True)
    turned = call(turn_kernel, [VM, VM], shape((AG_ROWS, SLOTS), F32))(recv.reshape(GRID, 2 * WID), line)
    gathered = lax.all_gather(turned.astype(jnp.float16), "etp", axis=0, tiled=True).reshape(N_ETP, AG_ROWS, SLOTS)
    lo = lax.dynamic_slice(gathered, (0, 0, 128 * core[0]), (N_ETP, AG_ROWS, 128)).astype(BF)
    hi = gathered[:, :, 256:].astype(BF)
    wg, wu, wd = own
    wg1, wu1, wd1 = (lax.ppermute(w, "etp", other) for w in own)
    partial = call(
        expert_kernel,
        [SM] + [VM] * 4 + [HBM] * 4,
        shape((N_ETP, WID * 3 // 2, 128), BF),
        scratch=[
            pltpu.VMEM((D, 256), BF),
            pltpu.VMEM((D, 256), BF),
            pltpu.VMEM((HID, D), BF),
            pltpu.VMEM((D, HID), BF),
            pltpu.VMEM((D, HID), BF),
            pltpu.VMEM((HID, D), BF),
            pltpu.SemaphoreType.DMA((4,)),
        ],
        vmem=24 << 20,
        cost=pl.CostEstimate(flops=10 * D * 512 * 256, bytes_accessed=12 << 20, transcendentals=512 * 256),
    )(core, lo, hi, wg1, wu1, *map(in_hbm, (wd1, wg, wu, wd)))
    parts = lax.all_to_all(partial, "etp", split_axis=0, concat_axis=0, tiled=True)
    summed = call(sum_kernel, [VM], shape((GRID, WID), BF))(parts)
    back = lax.all_to_all(summed.reshape(EXPERTS, ROWS, WID), "ep", split_axis=0, concat_axis=0, tiled=True)
    out = call(unpack_kernel, [VM] * 2, shape((WID, TOK), BF))(slot, back.reshape(GRID, WID))
    return out.T


def solution(mesh):
    placed = (
        P("ep", "etp"),
        P("ep", "etp"),
        P("ep", None),
        P("etp", None),
        P("ep", None, "etp"),
        P("ep", None, "etp"),
        P("ep", "etp", None),
    )
    return jax.shard_map(body, mesh=mesh, in_specs=placed, out_specs=P("ep", "etp"), check_vma=False)
```

```python
import jax
import jax.numpy as jnp
from jax import lax
from jax.experimental import pallas as pl
from jax.experimental.pallas import tpu as pltpu
from jax.sharding import PartitionSpec as P

CAP = 12
ROWS = 16
EXPERTS = 32
TOK = 256
WID = 160
N_ETP = 16
D = WID * N_ETP
HID = 256
SLOTS = EXPERTS * CAP
HALF = SLOTS // 2
GRID = EXPERTS * ROWS
AG_ROWS = 2 * WID + 8
F32 = jnp.float32
BF = jnp.bfloat16


def iota(shape, dim):
    return lax.broadcasted_iota(jnp.int32, shape, dim)


def dot(left, right, dims):
    return lax.dot_general(left, right, ((dims[:1], dims[1:]), ((), ())), preferred_element_type=F32)


def lane_slots():
    lane = iota((1, SLOTS), 1)
    half = jnp.where(lane < 256, lane // 128, lane // 64 % 2)
    at = jnp.where(lane < 256, lane % 128, 128 + lane % 64)
    return half * (EXPERTS // 2) + at // CAP, at % CAP


def slot_lanes():
    src, rank = lane_slots()
    return (iota((GRID, SLOTS), 0) == src * ROWS + rank).astype(BF)


def power(k):
    size, out = jnp.abs(k).astype(jnp.int32), jnp.ones_like(k)
    for bit in range(7):
        factor = jnp.where(k < 0, 2.0 ** -(1 << bit), 2.0 ** (1 << bit))
        out = jnp.where((size & (1 << bit)) != 0, out * factor, out)
    return out


def level(top):
    return 14.0 - jnp.clip(jnp.floor(jnp.log2(jnp.maximum(top, 1e-36))), -110.0, 14.0)


def pack_kernel(me_ref, ids_ref, x_ref, g_ref, router_ref, send_ref, slot_ref, line_ref, ids_v, x_v, g_v, router_v, sems):
    copies = [
        pltpu.make_async_copy(src, dst, sems.at[i])
        for i, (src, dst) in enumerate(((ids_ref, ids_v), (x_ref, x_v), (g_ref, g_v), (router_ref, router_v)))
    ]
    for c in copies:
        c.start()
    for c in copies:
        c.wait()
    mine = (iota((8, EXPERTS), 1) == me_ref[0]).astype(BF)
    column = dot(mine, router_v[...], (1, 0))
    shift = level(jnp.max(jnp.abs(column), axis=1, keepdims=True))
    scaled = column * power(shift)
    row = jnp.concatenate([scaled[:, :128], scaled[:, :128], scaled[:, 128:], jnp.zeros((8, 96), F32)], axis=1)
    line_ref[...] = jnp.where(iota((8, SLOTS), 0) == 0, row, jnp.broadcast_to(shift, (8, SLOTS)))
    ids = ids_v[...]
    picked = iota((EXPERTS, TOK), 0) == ids
    before = (iota((TOK, TOK), 0) < iota((TOK, TOK), 1)).astype(BF)
    earlier = dot(picked.astype(BF), before, (1, 0))
    rank = jnp.sum(jnp.where(picked, earlier, 0.0), axis=0, keepdims=True).astype(jnp.int32)
    slot = ids * ROWS + rank
    slot_ref[...] = slot
    place = (iota((GRID, TOK), 0) == slot).astype(BF)
    both = jnp.concatenate([x_v[...], g_v[...]], axis=0)
    send_ref[...] = dot(place, both, (1, 1)).astype(BF)


def turn_kernel(recv_ref, router_ref, out_ref):
    both = dot(recv_ref[...], slot_lanes(), (0, 0))
    shifts = []
    for i in range(2):
        half = both[i * WID : (i + 1) * WID]
        shift = level(jnp.max(jnp.abs(half), axis=0, keepdims=True))
        out_ref[i * WID : (i + 1) * WID, :] = half * power(shift)
        shifts.append(shift)
    row = iota((8, SLOTS), 0)
    out_ref[2 * WID :, :] = jnp.where(row < 2, router_ref[...], jnp.where(row == 2, shifts[0], shifts[1]))


def expert_kernel(core_ref, lo_ref, hi_ref, wg0, wu0, wd_other, wg_own, wu_own, wd_own, out_ref, x_ref, g_ref, wd0, wg1, wu1, wd1, sems):
    copies = []
    for i, (src, dst) in enumerate(((wd_other, wd0), (wg_own, wg1), (wu_own, wu1), (wd_own, wd1))):
        size = dst.shape[0] // 2
        parts = [pl.ds(p * size, size) for p in range(2)]
        copies.append([pltpu.make_async_copy(src.at[at], dst.at[at], sems.at[i, p]) for p, at in enumerate(parts)])
    for group in copies:
        for c in group:
            c.start()

    def rows(first, count):
        return jnp.concatenate([lo_ref[:, first : first + count, :], hi_ref[:, first : first + count, :]], axis=2)

    extra = rows(2 * WID, 8).astype(F32)
    back = power(-extra)
    logit = jnp.zeros((1, 256), F32)
    columns = []
    for j in range(N_ETP):
        at = pl.ds(j * WID, WID)
        for first, ref, row in ((0, x_ref, 2), (WID, g_ref, 3)):
            scale = back[j, row : row + 1, :].astype(BF)
            ref[at, :128] = lo_ref[j, first : first + WID, :] * scale[:, :128]
            ref[at, 128:] = hi_ref[j, first : first + WID, :] * scale[:, 128:]
        line = (extra[j, :8] * back[j, 1:2])[:, :WID]
        column = line.T[:, :1]
        logit += jnp.sum(x_ref[at, :].astype(F32) * column, axis=0, keepdims=True)
        columns.append(column)
    score = 1.0 / (1.0 + jnp.exp(-logit))
    xt = x_ref[...].T
    g = g_ref[...]
    d_gate, d_up = [], []
    d_score = jnp.zeros((1, 256), F32)
    for h, (wg, wu, wd) in enumerate(((wg0, wu0, wd0), (wg1, wu1, wd1))):
        for c in sum(copies[1:], []) if h else copies[0]:
            c.wait()
        gate = dot(xt, wg[...], (1, 0)).T
        up = dot(xt, wu[...], (1, 0)).T
        d_hidden = dot(wd[...], g, (1, 0))
        gate_pre, up_pre = gate * score, up * score
        sig = 1.0 / (1.0 + jnp.exp(-gate_pre))
        dg = (d_hidden * up_pre * (sig * (1.0 + gate_pre * (1.0 - sig)))).astype(BF)
        du = (d_hidden * (gate_pre * sig)).astype(BF)
        d_score += jnp.sum(dg.astype(F32) * gate + du.astype(F32) * up, axis=0, keepdims=True)
        d_gate.append(dg)
        d_up.append(du)
    d_logit = d_score * score * (1.0 - score)
    keep = (iota((WID // 2, 128), 1) // 64) == core_ref[0]
    for j in range(N_ETP):
        at = pl.ds(j * WID, WID)
        total = dot(wg0[at, :], d_gate[0], (1, 0)) + dot(wg1[at, :], d_gate[1], (1, 0))
        total += dot(wu0[at, :], d_up[0], (1, 0)) + dot(wu1[at, :], d_up[1], (1, 0))
        total = total * score + columns[j] * d_logit
        out_ref[j, :WID, :] = total[:, :128].astype(BF)
        top, bottom = total[: WID // 2, 128:], total[WID // 2 :, 128:]
        out_ref[j, WID:, :] = jnp.where(keep, top, pltpu.roll(bottom, 64, 1)).astype(BF)


def sum_kernel(recv_ref, out_ref):
    parts = []
    for c in range(2):
        total = recv_ref[c].astype(F32)
        for y in range(1, N_ETP // 2):
            total += recv_ref[2 * y + c].astype(F32)
        parts.append(total)
    first = iota((WID // 2, 128), 1) < 64
    top = jnp.where(first, parts[0][WID:], parts[1][WID:])
    bottom = jnp.where(first, pltpu.roll(parts[0][WID:], 64, 1), pltpu.roll(parts[1][WID:], 64, 1))
    whole = jnp.concatenate([parts[0][:WID], parts[1][:WID], jnp.concatenate([top, bottom], axis=0)], axis=1).astype(BF)
    src, rank = lane_slots()
    last = whole[128:]
    quarters = jnp.concatenate([jnp.where(rank % 4 == i, last, jnp.zeros_like(last)) for i in range(4)], axis=0)
    row = iota((GRID, SLOTS), 0)
    heads = (row == src * ROWS + rank).astype(BF)
    tails = (row == src * ROWS + CAP + rank // 4).astype(BF)
    out_ref[...] = (dot(heads, whole[:128], (1, 1)) + dot(tails, quarters, (1, 1))).astype(BF)


def unpack_kernel(slot_ref, recv_ref, out_ref):
    slot, row = slot_ref[...], iota((GRID, TOK), 0)
    rank = slot % ROWS
    heads = (row == slot).astype(BF)
    tails = (row == slot - rank + CAP + rank // 4).astype(BF)
    out_ref[:128, :] = dot(recv_ref[...], heads, (0, 0)).astype(BF)
    quarters = dot(recv_ref[...], tails, (0, 0))
    last = quarters[:32]
    for i in range(1, 4):
        last = jnp.where(rank % 4 == i, quarters[32 * i : 32 * (i + 1)], last)
    out_ref[128:, :] = last.astype(BF)


VM = pl.BlockSpec(memory_space=pltpu.VMEM)
SM = pl.BlockSpec(memory_space=pltpu.SMEM)
HBM = pl.BlockSpec(memory_space=pltpu.HBM)


def in_hbm(x):
    return pltpu.with_memory_space_constraint(x, pltpu.HBM)


def call(kernel, ins, outs, out_specs=VM, scratch=(), vmem=32 << 20, cost=None):
    return pl.pallas_call(
        kernel,
        out_shape=outs,
        in_specs=ins,
        out_specs=out_specs,
        scratch_shapes=list(scratch),
        cost_estimate=cost,
        compiler_params=pltpu.CompilerParams(vmem_limit_bytes=vmem),
    )


def expert_call(core, lo, hi, wg1, wu1, wd1, wg, wu, wd):
    shape = jax.ShapeDtypeStruct
    return call(
        expert_kernel,
        [SM] + [VM] * 4 + [HBM] * 4,
        shape((N_ETP, WID * 3 // 2, 128), BF),
        scratch=[
            pltpu.VMEM((D, 256), BF),
            pltpu.VMEM((D, 256), BF),
            pltpu.VMEM((HID, D), BF),
            pltpu.VMEM((D, HID), BF),
            pltpu.VMEM((D, HID), BF),
            pltpu.VMEM((HID, D), BF),
            pltpu.SemaphoreType.DMA((4, 2)),
        ],
        vmem=24 << 20,
        cost=pl.CostEstimate(flops=10 * D * 512 * 256, bytes_accessed=12 << 20, transcendentals=512 * 256),
    )(core, lo, hi, wg1, wu1, *map(in_hbm, (wd1, wg, wu, wd)))


def body(tokens, grad_out, expert_ids, router, gate_weight, up_weight, down_weight):
    me = lax.axis_index("ep").astype(jnp.int32).reshape(1)
    core = (lax.axis_index("etp") % 2).astype(jnp.int32).reshape(1)
    other = [(i, i ^ 1) for i in range(N_ETP)]
    own = [gate_weight[0], up_weight[0], down_weight[0]]
    shape = jax.ShapeDtypeStruct

    send, slot, line = call(
        pack_kernel,
        [SM] + [HBM] * 4,
        [shape((GRID, 2 * WID), BF), shape((1, TOK), jnp.int32), shape((8, SLOTS), F32)],
        [VM] * 3,
        [
            pltpu.VMEM((1, TOK), jnp.int32),
            pltpu.VMEM((WID, TOK), BF),
            pltpu.VMEM((WID, TOK), BF),
            pltpu.VMEM((EXPERTS, WID), BF),
            pltpu.SemaphoreType.DMA((4,)),
        ],
    )(me, *map(in_hbm, (expert_ids.reshape(1, TOK), tokens.T, grad_out.T, router.T)))
    recv = lax.all_to_all(send.reshape(EXPERTS, ROWS, 2 * WID), "ep", split_axis=0, concat_axis=0, tiled=True)
    turned = call(turn_kernel, [VM, VM], shape((AG_ROWS, SLOTS), F32))(recv.reshape(GRID, 2 * WID), line)
    gathered = lax.all_gather(turned.astype(jnp.float16), "etp", axis=0, tiled=True).reshape(N_ETP, AG_ROWS, SLOTS)
    lo = lax.dynamic_slice(gathered, (0, 0, 128 * core[0]), (N_ETP, AG_ROWS, 128)).astype(BF)
    hi = gathered[:, :, 256:].astype(BF)
    wg, wu, wd = own
    wg1, wu1, wd1 = (lax.ppermute(w, "etp", other) for w in own)
    partial = expert_call(core, lo, hi, wg1, wu1, wd1, wg, wu, wd)
    parts = lax.all_to_all(partial, "etp", split_axis=0, concat_axis=0, tiled=True)
    summed = call(sum_kernel, [VM], shape((GRID, 128), BF))(parts)
    back = lax.all_to_all(summed.reshape(EXPERTS, ROWS, 128), "ep", split_axis=0, concat_axis=0, tiled=True)
    out = call(unpack_kernel, [VM] * 2, shape((WID, TOK), BF))(slot, back.reshape(GRID, 128))
    return out.T


def solution(mesh):
    placed = (
        P("ep", "etp"),
        P("ep", "etp"),
        P("ep", None),
        P("etp", None),
        P("ep", None, "etp"),
        P("ep", None, "etp"),
        P("ep", "etp", None),
    )
    return jax.shard_map(body, mesh=mesh, in_specs=placed, out_specs=P("ep", "etp"), check_vma=False)
```

```python
import jax
import jax.numpy as jnp
from jax import lax
from jax.experimental import pallas as pl
from jax.experimental.pallas import tpu as pltpu
from jax.sharding import PartitionSpec as P

CAP = 12
ROWS = 16
EXPERTS = 32
TOK = 256
WID = 160
N_ETP = 16
D = WID * N_ETP
HID = 256
SLOTS = EXPERTS * CAP
HALF = SLOTS // 2
GRID = EXPERTS * ROWS
AG_ROWS = 2 * WID + 8
F32 = jnp.float32
BF = jnp.bfloat16


def iota(shape, dim):
    return lax.broadcasted_iota(jnp.int32, shape, dim)


def dot(left, right, dims):
    return lax.dot_general(left, right, ((dims[:1], dims[1:]), ((), ())), preferred_element_type=F32)


def lane_slots():
    lane = iota((1, SLOTS), 1)
    half = jnp.where(lane < 256, lane // 128, lane // 64 % 2)
    at = jnp.where(lane < 256, lane % 128, 128 + lane % 64)
    return half * (EXPERTS // 2) + at // CAP, at % CAP


def slot_lanes():
    src, rank = lane_slots()
    return (iota((GRID, SLOTS), 0) == src * ROWS + rank).astype(BF)


def power(k):
    size, out = jnp.abs(k).astype(jnp.int32), jnp.ones_like(k)
    for bit in range(7):
        factor = jnp.where(k < 0, 2.0 ** -(1 << bit), 2.0 ** (1 << bit))
        out = jnp.where((size & (1 << bit)) != 0, out * factor, out)
    return out


def level(top):
    return 14.0 - jnp.clip(jnp.floor(jnp.log2(jnp.maximum(top, 1e-36))), -110.0, 14.0)


def pack_kernel(me_ref, ids_ref, x_ref, g_ref, router_ref, send_ref, slot_ref, line_ref, ids_v, x_v, g_v, router_v, sems):
    copies = [
        pltpu.make_async_copy(src, dst, sems.at[i])
        for i, (src, dst) in enumerate(((ids_ref, ids_v), (x_ref, x_v), (g_ref, g_v), (router_ref, router_v)))
    ]
    for c in copies:
        c.start()
    copies[0].wait()
    copies[3].wait()
    mine = (iota((8, EXPERTS), 1) == me_ref[0]).astype(BF)
    column = dot(mine, router_v[...], (1, 0))
    shift = level(jnp.max(jnp.abs(column), axis=1, keepdims=True))
    scaled = column * power(shift)
    row = jnp.concatenate([scaled[:, :128], scaled[:, :128], scaled[:, 128:], jnp.zeros((8, 96), F32)], axis=1)
    line_ref[...] = jnp.where(iota((8, SLOTS), 0) == 0, row, jnp.broadcast_to(shift, (8, SLOTS)))
    ids = ids_v[...]
    picked = iota((EXPERTS, TOK), 0) == ids
    before = (iota((TOK, TOK), 0) < iota((TOK, TOK), 1)).astype(BF)
    earlier = dot(picked.astype(BF), before, (1, 0))
    rank = jnp.sum(jnp.where(picked, earlier, 0.0), axis=0, keepdims=True).astype(jnp.int32)
    slot = ids * ROWS + rank
    slot_ref[...] = slot
    place = (iota((GRID, TOK), 0) == slot).astype(BF)
    copies[1].wait()
    copies[2].wait()
    both = jnp.concatenate([x_v[...], g_v[...]], axis=0)
    send_ref[...] = dot(place, both, (1, 1)).astype(BF)


def turn_kernel(recv_ref, router_ref, out_ref):
    both = dot(recv_ref[...], slot_lanes(), (0, 0))
    shifts = []
    for i in range(2):
        half = both[i * WID : (i + 1) * WID]
        shift = level(jnp.max(jnp.abs(half), axis=0, keepdims=True))
        out_ref[i * WID : (i + 1) * WID, :] = half * power(shift)
        shifts.append(shift)
    row = iota((8, SLOTS), 0)
    out_ref[2 * WID :, :] = jnp.where(row < 2, router_ref[...], jnp.where(row == 2, shifts[0], shifts[1]))


def prepare_kernel(lo_ref, hi_ref, wd_ref, xt_ref, g_ref, score_ref, router_ref, wd_out, x_ref, sems):
    size = HID // 2
    copies = []
    for p in range(2):
        at = pl.ds(p * size, size)
        copies.append(pltpu.make_async_copy(wd_ref.at[at], wd_out.at[at], sems.at[p]))
    for c in copies:
        c.start()

    def rows(first, count):
        return jnp.concatenate([lo_ref[:, first : first + count, :], hi_ref[:, first : first + count, :]], axis=2)

    extra = rows(2 * WID, 8).astype(F32)
    back = power(-extra)
    lines = jnp.concatenate([extra[j, :1] * back[j, 1:2] for j in range(N_ETP)], axis=0)[:, :WID]
    columns = lines.T
    router_ref[...] = columns
    logit = jnp.zeros((N_ETP, 256), F32)
    narrow = lines.astype(BF)
    for j in range(N_ETP):
        at = pl.ds(j * WID, WID)
        for first, ref, row in ((0, x_ref, 2), (WID, g_ref, 3)):
            scale = back[j, row : row + 1, :].astype(BF)
            ref[at, :128] = lo_ref[j, first : first + WID, :] * scale[:, :128]
            ref[at, 128:] = hi_ref[j, first : first + WID, :] * scale[:, 128:]
        logit += jnp.where(iota((N_ETP, 256), 0) == j, dot(narrow, x_ref[at, :], (1, 0)), 0.0)
    logit = jnp.sum(logit, axis=0, keepdims=True)
    score_ref[...] = 1.0 / (1.0 + jnp.exp(-logit))
    xt_ref[...] = x_ref[...].T
    for c in copies:
        c.wait()


def expert_kernel(core_ref, xt_ref, g_ref, score_ref, router_ref, wg0, wu0, wd0, wg1, wu1, wd1, out_ref):
    score, xt, g = score_ref[...], xt_ref[...], g_ref[...]
    d_gate, d_up = [], []
    d_score = jnp.zeros((1, 256), F32)
    for wg, wu, wd in ((wg0, wu0, wd0), (wg1, wu1, wd1)):
        gate = dot(xt, wg[...], (1, 0)).T
        up = dot(xt, wu[...], (1, 0)).T
        d_hidden = dot(wd[...], g, (1, 0))
        gate_pre, up_pre = gate * score, up * score
        sig = 1.0 / (1.0 + jnp.exp(-gate_pre))
        dg = (d_hidden * up_pre * (sig * (1.0 + gate_pre * (1.0 - sig)))).astype(BF)
        du = (d_hidden * (gate_pre * sig)).astype(BF)
        d_score += jnp.sum(dg.astype(F32) * gate + du.astype(F32) * up, axis=0, keepdims=True)
        d_gate.append(dg)
        d_up.append(du)
    d_logit = d_score * score * (1.0 - score)
    keep = (iota((WID // 2, 128), 1) // 64) == core_ref[0]
    for j in range(N_ETP):
        at = pl.ds(j * WID, WID)
        total = dot(wg0[at, :], d_gate[0], (1, 0)) + dot(wg1[at, :], d_gate[1], (1, 0))
        total += dot(wu0[at, :], d_up[0], (1, 0)) + dot(wu1[at, :], d_up[1], (1, 0))
        total = total * score + router_ref[:, j : j + 1] * d_logit
        out_ref[j, :WID, :] = total[:, :128].astype(BF)
        top, bottom = total[: WID // 2, 128:], total[WID // 2 :, 128:]
        out_ref[j, WID:, :] = jnp.where(keep, top, pltpu.roll(bottom, 64, 1)).astype(BF)


def sum_kernel(recv_ref, out_ref):
    parts = []
    for c in range(2):
        total = recv_ref[c].astype(F32)
        for y in range(1, N_ETP // 2):
            total += recv_ref[2 * y + c].astype(F32)
        parts.append(total)
    first = iota((WID // 2, 128), 1) < 64
    top = jnp.where(first, parts[0][WID:], parts[1][WID:])
    bottom = jnp.where(first, pltpu.roll(parts[0][WID:], 64, 1), pltpu.roll(parts[1][WID:], 64, 1))
    whole = jnp.concatenate([parts[0][:WID], parts[1][:WID], jnp.concatenate([top, bottom], axis=0)], axis=1).astype(BF)
    src, rank = lane_slots()
    last = whole[128:]
    quarters = jnp.concatenate([jnp.where(rank % 4 == i, last, jnp.zeros_like(last)) for i in range(4)], axis=0)
    row = iota((GRID, SLOTS), 0)
    heads = (row == src * ROWS + rank).astype(BF)
    tails = (row == src * ROWS + CAP + rank // 4).astype(BF)
    out_ref[...] = (dot(heads, whole[:128], (1, 1)) + dot(tails, quarters, (1, 1))).astype(BF)


def unpack_kernel(slot_ref, recv_ref, out_ref):
    slot, row = slot_ref[...], iota((GRID, TOK), 0)
    rank = slot % ROWS
    heads = (row == slot).astype(BF)
    tails = (row == slot - rank + CAP + rank // 4).astype(BF)
    out_ref[:128, :] = dot(recv_ref[...], heads, (0, 0)).astype(BF)
    quarters = dot(recv_ref[...], tails, (0, 0))
    last = quarters[:32]
    for i in range(1, 4):
        last = jnp.where(rank % 4 == i, quarters[32 * i : 32 * (i + 1)], last)
    out_ref[128:, :] = last.astype(BF)


VM = pl.BlockSpec(memory_space=pltpu.VMEM)
SM = pl.BlockSpec(memory_space=pltpu.SMEM)
HBM = pl.BlockSpec(memory_space=pltpu.HBM)


def in_hbm(x):
    return pltpu.with_memory_space_constraint(x, pltpu.HBM)


def call(kernel, ins, outs, out_specs=VM, scratch=(), vmem=32 << 20, cost=None):
    return pl.pallas_call(
        kernel,
        out_shape=outs,
        in_specs=ins,
        out_specs=out_specs,
        scratch_shapes=list(scratch),
        cost_estimate=cost,
        compiler_params=pltpu.CompilerParams(vmem_limit_bytes=vmem),
    )


def expert_call(core, lo, hi, wg1, wu1, wd1, wg, wu, wd):
    shape = jax.ShapeDtypeStruct
    xt, g, score, columns, wd1 = call(
        prepare_kernel,
        [VM] * 2 + [HBM],
        [
            shape((256, D), BF),
            shape((D, 256), BF),
            shape((1, 256), F32),
            shape((WID, N_ETP), F32),
            pltpu.VMEM((HID, D), BF),
        ],
        [VM] * 5,
        [pltpu.VMEM((D, 256), BF), pltpu.SemaphoreType.DMA((2,))],
        vmem=16 << 20,
    )(lo, hi, in_hbm(wd1))
    return call(
        expert_kernel,
        [SM] + [VM] * 10,
        shape((N_ETP, WID * 3 // 2, 128), BF),
        vmem=20 << 20,
        cost=pl.CostEstimate(flops=10 * D * 512 * 256, bytes_accessed=12 << 20, transcendentals=512 * 256),
    )(core, xt, g, score, columns, wg1, wu1, wd1, wg, wu, wd)


def body(tokens, grad_out, expert_ids, router, gate_weight, up_weight, down_weight):
    me = lax.axis_index("ep").astype(jnp.int32).reshape(1)
    core = (lax.axis_index("etp") % 2).astype(jnp.int32).reshape(1)
    other = [(i, i ^ 1) for i in range(N_ETP)]
    own = [gate_weight[0], up_weight[0], down_weight[0]]
    shape = jax.ShapeDtypeStruct

    send, slot, line = call(
        pack_kernel,
        [SM] + [HBM] * 4,
        [shape((GRID, 2 * WID), BF), shape((1, TOK), jnp.int32), shape((8, SLOTS), F32)],
        [VM] * 3,
        [
            pltpu.VMEM((1, TOK), jnp.int32),
            pltpu.VMEM((WID, TOK), BF),
            pltpu.VMEM((WID, TOK), BF),
            pltpu.VMEM((EXPERTS, WID), BF),
            pltpu.SemaphoreType.DMA((4,)),
        ],
    )(me, *map(in_hbm, (expert_ids.reshape(1, TOK), tokens.T, grad_out.T, router.T)))
    recv = lax.all_to_all(send.reshape(EXPERTS, ROWS, 2 * WID), "ep", split_axis=0, concat_axis=0, tiled=True)
    turned = call(turn_kernel, [VM, VM], shape((AG_ROWS, SLOTS), F32))(recv.reshape(GRID, 2 * WID), line)
    gathered = lax.all_gather(turned.astype(jnp.float16), "etp", axis=0, tiled=True).reshape(N_ETP, AG_ROWS, SLOTS)
    lo = lax.dynamic_slice(gathered, (0, 0, 128 * core[0]), (N_ETP, AG_ROWS, 128)).astype(BF)
    hi = gathered[:, :, 256:].astype(BF)
    wg, wu, wd = own
    wg1, wu1, wd1 = (lax.ppermute(w, "etp", other) for w in own)
    partial = expert_call(core, lo, hi, wg1, wu1, wd1, wg, wu, wd)
    parts = lax.all_to_all(partial, "etp", split_axis=0, concat_axis=0, tiled=True)
    summed = call(sum_kernel, [VM], shape((GRID, 128), BF))(parts)
    back = lax.all_to_all(summed.reshape(EXPERTS, ROWS, 128), "ep", split_axis=0, concat_axis=0, tiled=True)
    out = call(unpack_kernel, [VM] * 2, shape((WID, TOK), BF))(slot, back.reshape(GRID, 128))
    return out.T


def solution(mesh):
    placed = (
        P("ep", "etp"),
        P("ep", "etp"),
        P("ep", None),
        P("etp", None),
        P("ep", None, "etp"),
        P("ep", None, "etp"),
        P("ep", "etp", None),
    )
    return jax.shard_map(body, mesh=mesh, in_specs=placed, out_specs=P("ep", "etp"), check_vma=False)
```

```python
import jax
import jax.numpy as jnp
from jax import lax
from jax.experimental import pallas as pl
from jax.experimental.pallas import tpu as pltpu
from jax.sharding import PartitionSpec as P

CAP = 12
ROWS = 16
EXPERTS = 32
TOK = 256
WID = 160
N_ETP = 16
D = WID * N_ETP
HID = 256
SLOTS = EXPERTS * CAP
HALF = SLOTS // 2
GRID = EXPERTS * ROWS
AG_ROWS = 2 * WID + 8
F32 = jnp.float32
BF = jnp.bfloat16


ETP_ORDER = [2 * y + y % 2 for y in range(8)] + [2 * y + 1 - y % 2 for y in range(7, -1, -1)]
ETP_PLACE = [ETP_ORDER.index(i) for i in range(N_ETP)]
EP_ORDER = [4 * z + (x + z) % 4 for x in range(4) for z in range(8)]


def ep_place(i):
    z = i // 4
    return (i - z) % 4 * 8 + z


def iota(shape, dim):
    return lax.broadcasted_iota(jnp.int32, shape, dim)


def dot(left, right, dims):
    return lax.dot_general(left, right, ((dims[:1], dims[1:]), ((), ())), preferred_element_type=F32)


def lane_slots():
    lane = iota((1, SLOTS), 1)
    half = jnp.where(lane < 256, lane // 128, lane // 64 % 2)
    at = jnp.where(lane < 256, lane % 128, 128 + lane % 64)
    return half * (EXPERTS // 2) + at // CAP, at % CAP


def slot_lanes():
    src, rank = lane_slots()
    return (iota((GRID, SLOTS), 0) == src * ROWS + rank).astype(BF)


def power(k):
    size, out = jnp.abs(k).astype(jnp.int32), jnp.ones_like(k)
    for bit in range(7):
        factor = jnp.where(k < 0, 2.0 ** -(1 << bit), 2.0 ** (1 << bit))
        out = jnp.where((size & (1 << bit)) != 0, out * factor, out)
    return out


def level(top):
    return 14.0 - jnp.clip(jnp.floor(jnp.log2(jnp.maximum(top, 1e-36))), -110.0, 14.0)


def pack_kernel(me_ref, ids_ref, x_ref, g_ref, router_ref, send_ref, slot_ref, line_ref, ids_v, x_v, g_v, router_v, sems):
    copies = [
        pltpu.make_async_copy(src, dst, sems.at[i])
        for i, (src, dst) in enumerate(((ids_ref, ids_v), (x_ref, x_v), (g_ref, g_v), (router_ref, router_v)))
    ]
    for c in copies:
        c.start()
    copies[0].wait()
    copies[3].wait()
    mine = (iota((8, EXPERTS), 1) == me_ref[0]).astype(BF)
    column = dot(mine, router_v[...], (1, 0))
    shift = level(jnp.max(jnp.abs(column), axis=1, keepdims=True))
    scaled = column * power(shift)
    row = jnp.concatenate([scaled[:, :128], scaled[:, :128], scaled[:, 128:], jnp.zeros((8, 96), F32)], axis=1)
    line_ref[...] = jnp.where(iota((8, SLOTS), 0) == 0, row, jnp.broadcast_to(shift, (8, SLOTS)))
    ids = ids_v[...]
    picked = iota((EXPERTS, TOK), 0) == ids
    before = (iota((TOK, TOK), 0) < iota((TOK, TOK), 1)).astype(BF)
    earlier = dot(picked.astype(BF), before, (1, 0))
    rank = jnp.sum(jnp.where(picked, earlier, 0.0), axis=0, keepdims=True).astype(jnp.int32)
    slot = ep_place(ids) * ROWS + rank
    slot_ref[...] = slot
    place = (iota((GRID, TOK), 0) == slot).astype(BF)
    copies[1].wait()
    copies[2].wait()
    both = jnp.concatenate([x_v[...], g_v[...]], axis=0)
    send_ref[...] = dot(place, both, (1, 1)).astype(BF)


def turn_kernel(recv_ref, router_ref, out_ref):
    both = dot(recv_ref[...], slot_lanes(), (0, 0))
    shifts = []
    for i in range(2):
        half = both[i * WID : (i + 1) * WID]
        shift = level(jnp.max(jnp.abs(half), axis=0, keepdims=True))
        out_ref[i * WID : (i + 1) * WID, :] = half * power(shift)
        shifts.append(shift)
    row = iota((8, SLOTS), 0)
    out_ref[2 * WID :, :] = jnp.where(row < 2, router_ref[...], jnp.where(row == 2, shifts[0], shifts[1]))


def prepare_kernel(lo_ref, hi_ref, wd_ref, xt_ref, g_ref, score_ref, router_ref, wd_out, x_ref, sems):
    size = HID // 2
    copies = []
    for p in range(2):
        at = pl.ds(p * size, size)
        copies.append(pltpu.make_async_copy(wd_ref.at[at], wd_out.at[at], sems.at[p]))
    for c in copies:
        c.start()

    def rows(first, count):
        return jnp.concatenate([lo_ref[:, first : first + count, :], hi_ref[:, first : first + count, :]], axis=2)

    extra = rows(2 * WID, 8).astype(F32)
    back = power(-extra)
    lines = jnp.concatenate([extra[j, :1] * back[j, 1:2] for j in range(N_ETP)], axis=0)[:, :WID]
    columns = lines.T
    router_ref[...] = columns
    logit = jnp.zeros((N_ETP, 256), F32)
    narrow = lines.astype(BF)
    for j in range(N_ETP):
        at = pl.ds(j * WID, WID)
        for first, ref, row in ((0, x_ref, 2), (WID, g_ref, 3)):
            scale = back[j, row : row + 1, :].astype(BF)
            ref[at, :128] = lo_ref[j, first : first + WID, :] * scale[:, :128]
            ref[at, 128:] = hi_ref[j, first : first + WID, :] * scale[:, 128:]
        logit += jnp.where(iota((N_ETP, 256), 0) == j, dot(narrow, x_ref[at, :], (1, 0)), 0.0)
    logit = jnp.sum(logit, axis=0, keepdims=True)
    score_ref[...] = 1.0 / (1.0 + jnp.exp(-logit))
    xt_ref[...] = x_ref[...].T
    for c in copies:
        c.wait()


def expert_kernel(core_ref, xt_ref, g_ref, score_ref, router_ref, wg0, wu0, wd0, wg1, wu1, wd1, out_ref):
    score, xt, g = score_ref[...], xt_ref[...], g_ref[...]
    d_gate, d_up = [], []
    d_score = jnp.zeros((1, 256), F32)
    for wg, wu, wd in ((wg0, wu0, wd0), (wg1, wu1, wd1)):
        gate = dot(xt, wg[...], (1, 0)).T
        up = dot(xt, wu[...], (1, 0)).T
        d_hidden = dot(wd[...], g, (1, 0))
        gate_pre, up_pre = gate * score, up * score
        sig = 1.0 / (1.0 + jnp.exp(-gate_pre))
        dg = (d_hidden * up_pre * (sig * (1.0 + gate_pre * (1.0 - sig)))).astype(BF)
        du = (d_hidden * (gate_pre * sig)).astype(BF)
        d_score += jnp.sum(dg.astype(F32) * gate + du.astype(F32) * up, axis=0, keepdims=True)
        d_gate.append(dg)
        d_up.append(du)
    d_logit = d_score * score * (1.0 - score)
    keep = (iota((WID // 2, 128), 1) // 64) == core_ref[0]
    for j in range(N_ETP):
        at = pl.ds(j * WID, WID)
        total = dot(wg0[at, :], d_gate[0], (1, 0)) + dot(wg1[at, :], d_gate[1], (1, 0))
        total += dot(wu0[at, :], d_up[0], (1, 0)) + dot(wu1[at, :], d_up[1], (1, 0))
        total = total * score + router_ref[:, j : j + 1] * d_logit
        out_ref[ETP_PLACE[j], :WID, :] = total[:, :128].astype(BF)
        top, bottom = total[: WID // 2, 128:], total[WID // 2 :, 128:]
        out_ref[ETP_PLACE[j], WID:, :] = jnp.where(keep, top, pltpu.roll(bottom, 64, 1)).astype(BF)


def sum_kernel(recv_ref, out_ref):
    parts = []
    for c in range(2):
        total = recv_ref[ETP_PLACE[c]].astype(F32)
        for y in range(1, N_ETP // 2):
            total += recv_ref[ETP_PLACE[2 * y + c]].astype(F32)
        parts.append(total)
    first = iota((WID // 2, 128), 1) < 64
    top = jnp.where(first, parts[0][WID:], parts[1][WID:])
    bottom = jnp.where(first, pltpu.roll(parts[0][WID:], 64, 1), pltpu.roll(parts[1][WID:], 64, 1))
    whole = jnp.concatenate([parts[0][:WID], parts[1][:WID], jnp.concatenate([top, bottom], axis=0)], axis=1).astype(BF)
    src, rank = lane_slots()
    last = whole[128:]
    quarters = jnp.concatenate([jnp.where(rank % 4 == i, last, jnp.zeros_like(last)) for i in range(4)], axis=0)
    row = iota((GRID, SLOTS), 0)
    heads = (row == src * ROWS + rank).astype(BF)
    tails = (row == src * ROWS + CAP + rank // 4).astype(BF)
    out_ref[...] = (dot(heads, whole[:128], (1, 1)) + dot(tails, quarters, (1, 1))).astype(BF)


def unpack_kernel(slot_ref, recv_ref, out_ref):
    slot, row = slot_ref[...], iota((GRID, TOK), 0)
    rank = slot % ROWS
    heads = (row == slot).astype(BF)
    tails = (row == slot - rank + CAP + rank // 4).astype(BF)
    out_ref[:128, :] = dot(recv_ref[...], heads, (0, 0)).astype(BF)
    quarters = dot(recv_ref[...], tails, (0, 0))
    last = quarters[:32]
    for i in range(1, 4):
        last = jnp.where(rank % 4 == i, quarters[32 * i : 32 * (i + 1)], last)
    out_ref[128:, :] = last.astype(BF)


VM = pl.BlockSpec(memory_space=pltpu.VMEM)
SM = pl.BlockSpec(memory_space=pltpu.SMEM)
HBM = pl.BlockSpec(memory_space=pltpu.HBM)


def in_hbm(x):
    return pltpu.with_memory_space_constraint(x, pltpu.HBM)


def call(kernel, ins, outs, out_specs=VM, scratch=(), vmem=32 << 20, cost=None):
    return pl.pallas_call(
        kernel,
        out_shape=outs,
        in_specs=ins,
        out_specs=out_specs,
        scratch_shapes=list(scratch),
        cost_estimate=cost,
        compiler_params=pltpu.CompilerParams(vmem_limit_bytes=vmem),
    )


def expert_call(core, lo, hi, wg1, wu1, wd1, wg, wu, wd):
    shape = jax.ShapeDtypeStruct
    xt, g, score, columns, wd1 = call(
        prepare_kernel,
        [VM] * 2 + [HBM],
        [
            shape((256, D), BF),
            shape((D, 256), BF),
            shape((1, 256), F32),
            shape((WID, N_ETP), F32),
            pltpu.VMEM((HID, D), BF),
        ],
        [VM] * 5,
        [pltpu.VMEM((D, 256), BF), pltpu.SemaphoreType.DMA((2,))],
        vmem=16 << 20,
    )(lo, hi, in_hbm(wd1))
    return call(
        expert_kernel,
        [SM] + [VM] * 10,
        shape((N_ETP, WID * 3 // 2, 128), BF),
        vmem=20 << 20,
        cost=pl.CostEstimate(flops=10 * D * 512 * 256, bytes_accessed=12 << 20, transcendentals=512 * 256),
    )(core, xt, g, score, columns, wg1, wu1, wd1, wg, wu, wd)


def body(tokens, grad_out, expert_ids, router, gate_weight, up_weight, down_weight):
    me = lax.axis_index("ep").astype(jnp.int32).reshape(1)
    core = (lax.axis_index("etp") % 2).astype(jnp.int32).reshape(1)
    other = [(i, i ^ 1) for i in range(N_ETP)]
    own = [gate_weight[0], up_weight[0], down_weight[0]]
    shape = jax.ShapeDtypeStruct

    send, slot, line = call(
        pack_kernel,
        [SM] + [HBM] * 4,
        [shape((GRID, 2 * WID), BF), shape((1, TOK), jnp.int32), shape((8, SLOTS), F32)],
        [VM] * 3,
        [
            pltpu.VMEM((1, TOK), jnp.int32),
            pltpu.VMEM((WID, TOK), BF),
            pltpu.VMEM((WID, TOK), BF),
            pltpu.VMEM((EXPERTS, WID), BF),
            pltpu.SemaphoreType.DMA((4,)),
        ],
    )(me, *map(in_hbm, (expert_ids.reshape(1, TOK), tokens.T, grad_out.T, router.T)))
    recv = lax.all_to_all(send.reshape(EXPERTS, ROWS, 2 * WID), "ep", split_axis=0, concat_axis=0, tiled=True, axis_index_groups=[EP_ORDER])
    turned = call(turn_kernel, [VM, VM], shape((AG_ROWS, SLOTS), F32))(recv.reshape(GRID, 2 * WID), line)
    gathered = lax.all_gather(turned.astype(jnp.float16), "etp", axis=0, tiled=True).reshape(N_ETP, AG_ROWS, SLOTS)
    lo = lax.dynamic_slice(gathered, (0, 0, 128 * core[0]), (N_ETP, AG_ROWS, 128)).astype(BF)
    hi = gathered[:, :, 256:].astype(BF)
    wg, wu, wd = own
    wg1, wu1, wd1 = (lax.ppermute(w, "etp", other) for w in own)
    partial = expert_call(core, lo, hi, wg1, wu1, wd1, wg, wu, wd)
    parts = lax.all_to_all(partial, "etp", split_axis=0, concat_axis=0, tiled=True, axis_index_groups=[ETP_ORDER])
    summed = call(sum_kernel, [VM], shape((GRID, 128), BF))(parts)
    back = lax.all_to_all(summed.reshape(EXPERTS, ROWS, 128), "ep", split_axis=0, concat_axis=0, tiled=True, axis_index_groups=[EP_ORDER])
    out = call(unpack_kernel, [VM] * 2, shape((WID, TOK), BF))(slot, back.reshape(GRID, 128))
    return out.T


def solution(mesh):
    placed = (
        P("ep", "etp"),
        P("ep", "etp"),
        P("ep", None),
        P("etp", None),
        P("ep", None, "etp"),
        P("ep", None, "etp"),
        P("ep", "etp", None),
    )
    return jax.shard_map(body, mesh=mesh, in_specs=placed, out_specs=P("ep", "etp"), check_vma=False)
```

```python
import jax
import jax.numpy as jnp
from jax import lax
from jax.experimental import pallas as pl
from jax.experimental.pallas import tpu as pltpu
from jax.sharding import PartitionSpec as P

CAP = 12
ROWS = 16
EXPERTS = 32
TOK = 256
WID = 160
N_ETP = 16
D = WID * N_ETP
HID = 256
SLOTS = EXPERTS * CAP
HALF = SLOTS // 2
GRID = EXPERTS * ROWS
AG_ROWS = 2 * WID + 8
F32 = jnp.float32
BF = jnp.bfloat16


ETP_ORDER = [2 * y + y % 2 for y in range(8)] + [2 * y + 1 - y % 2 for y in range(8)]
ETP_PLACE = [ETP_ORDER.index(i) for i in range(N_ETP)]
EP_ORDER = [4 * z + (x + z) % 4 for x in range(4) for z in range(8)]


def ep_place(i):
    z = i // 4
    return (i - z) % 4 * 8 + z


def iota(shape, dim):
    return lax.broadcasted_iota(jnp.int32, shape, dim)


def dot(left, right, dims):
    return lax.dot_general(left, right, ((dims[:1], dims[1:]), ((), ())), preferred_element_type=F32)


def lane_slots():
    lane = iota((1, SLOTS), 1)
    half = jnp.where(lane < 256, lane // 128, lane // 64 % 2)
    at = jnp.where(lane < 256, lane % 128, 128 + lane % 64)
    return half * (EXPERTS // 2) + at // CAP, at % CAP


def slot_lanes():
    src, rank = lane_slots()
    return (iota((GRID, SLOTS), 0) == src * ROWS + rank).astype(BF)


def power(k):
    size, out = jnp.abs(k).astype(jnp.int32), jnp.ones_like(k)
    for bit in range(7):
        factor = jnp.where(k < 0, 2.0 ** -(1 << bit), 2.0 ** (1 << bit))
        out = jnp.where((size & (1 << bit)) != 0, out * factor, out)
    return out


def level(top):
    return 14.0 - jnp.clip(jnp.floor(jnp.log2(jnp.maximum(top, 1e-36))), -110.0, 14.0)


def pack_kernel(me_ref, ids_ref, x_ref, g_ref, router_ref, send_ref, slot_ref, line_ref, ids_v, x_v, g_v, router_v, sems):
    copies = [
        pltpu.make_async_copy(src, dst, sems.at[i])
        for i, (src, dst) in enumerate(((ids_ref, ids_v), (x_ref, x_v), (g_ref, g_v), (router_ref, router_v)))
    ]
    for c in copies:
        c.start()
    copies[0].wait()
    copies[3].wait()
    mine = (iota((8, EXPERTS), 1) == me_ref[0]).astype(BF)
    column = dot(mine, router_v[...], (1, 0))
    shift = level(jnp.max(jnp.abs(column), axis=1, keepdims=True))
    scaled = column * power(shift)
    row = jnp.concatenate([scaled[:, :128], scaled[:, :128], scaled[:, 128:], jnp.zeros((8, 96), F32)], axis=1)
    line_ref[...] = jnp.where(iota((8, SLOTS), 0) == 0, row, jnp.broadcast_to(shift, (8, SLOTS)))
    ids = ids_v[...]
    picked = iota((EXPERTS, TOK), 0) == ids
    before = (iota((TOK, TOK), 0) < iota((TOK, TOK), 1)).astype(BF)
    earlier = dot(picked.astype(BF), before, (1, 0))
    rank = jnp.sum(jnp.where(picked, earlier, 0.0), axis=0, keepdims=True).astype(jnp.int32)
    slot = ep_place(ids) * ROWS + rank
    slot_ref[...] = slot
    place = (iota((GRID, TOK), 0) == slot).astype(BF)
    copies[1].wait()
    copies[2].wait()
    both = jnp.concatenate([x_v[...], g_v[...]], axis=0)
    send_ref[...] = dot(place, both, (1, 1)).astype(BF)


def turn_kernel(recv_ref, router_ref, out_ref):
    both = dot(recv_ref[...], slot_lanes(), (0, 0))
    shifts = []
    for i in range(2):
        half = both[i * WID : (i + 1) * WID]
        shift = level(jnp.max(jnp.abs(half), axis=0, keepdims=True))
        out_ref[i * WID : (i + 1) * WID, :] = half * power(shift)
        shifts.append(shift)
    row = iota((8, SLOTS), 0)
    out_ref[2 * WID :, :] = jnp.where(row < 2, router_ref[...], jnp.where(row == 2, shifts[0], shifts[1]))


def prepare_kernel(lo_ref, hi_ref, wd_ref, xt_ref, g_ref, score_ref, router_ref, wd_out, x_ref, sems):
    size = HID // 2
    copies = []
    for p in range(2):
        at = pl.ds(p * size, size)
        copies.append(pltpu.make_async_copy(wd_ref.at[at], wd_out.at[at], sems.at[p]))
    for c in copies:
        c.start()

    def rows(first, count):
        return jnp.concatenate([lo_ref[:, first : first + count, :], hi_ref[:, first : first + count, :]], axis=2)

    extra = rows(2 * WID, 8).astype(F32)
    back = power(-extra)
    lines = jnp.concatenate([extra[j, :1] * back[j, 1:2] for j in range(N_ETP)], axis=0)[:, :WID]
    columns = lines.T
    router_ref[...] = columns
    logit = jnp.zeros((N_ETP, 256), F32)
    narrow = lines.astype(BF)
    for j in range(N_ETP):
        at = pl.ds(j * WID, WID)
        for first, ref, row in ((0, x_ref, 2), (WID, g_ref, 3)):
            scale = back[j, row : row + 1, :].astype(BF)
            ref[at, :128] = lo_ref[j, first : first + WID, :] * scale[:, :128]
            ref[at, 128:] = hi_ref[j, first : first + WID, :] * scale[:, 128:]
        logit += jnp.where(iota((N_ETP, 256), 0) == j, dot(narrow, x_ref[at, :], (1, 0)), 0.0)
    logit = jnp.sum(logit, axis=0, keepdims=True)
    score_ref[...] = 1.0 / (1.0 + jnp.exp(-logit))
    xt_ref[...] = x_ref[...].T
    for c in copies:
        c.wait()


def expert_kernel(core_ref, xt_ref, g_ref, score_ref, router_ref, wg0, wu0, wd0, wg1, wu1, wd1, out_ref):
    score, xt, g = score_ref[...], xt_ref[...], g_ref[...]
    d_gate, d_up = [], []
    d_score = jnp.zeros((1, 256), F32)
    for wg, wu, wd in ((wg0, wu0, wd0), (wg1, wu1, wd1)):
        gate = dot(xt, wg[...], (1, 0)).T
        up = dot(xt, wu[...], (1, 0)).T
        d_hidden = dot(wd[...], g, (1, 0))
        gate_pre, up_pre = gate * score, up * score
        sig = 1.0 / (1.0 + jnp.exp(-gate_pre))
        dg = (d_hidden * up_pre * (sig * (1.0 + gate_pre * (1.0 - sig)))).astype(BF)
        du = (d_hidden * (gate_pre * sig)).astype(BF)
        d_score += jnp.sum(dg.astype(F32) * gate + du.astype(F32) * up, axis=0, keepdims=True)
        d_gate.append(dg)
        d_up.append(du)
    d_logit = d_score * score * (1.0 - score)
    keep = (iota((WID // 2, 128), 1) // 64) == core_ref[0]
    for j in range(N_ETP):
        at = pl.ds(j * WID, WID)
        total = dot(wg0[at, :], d_gate[0], (1, 0)) + dot(wg1[at, :], d_gate[1], (1, 0))
        total += dot(wu0[at, :], d_up[0], (1, 0)) + dot(wu1[at, :], d_up[1], (1, 0))
        total = total * score + router_ref[:, j : j + 1] * d_logit
        out_ref[ETP_PLACE[j], :WID, :] = total[:, :128].astype(BF)
        top, bottom = total[: WID // 2, 128:], total[WID // 2 :, 128:]
        out_ref[ETP_PLACE[j], WID:, :] = jnp.where(keep, top, pltpu.roll(bottom, 64, 1)).astype(BF)


def sum_kernel(recv_ref, out_ref):
    parts = []
    for c in range(2):
        total = recv_ref[ETP_PLACE[c]].astype(F32)
        for y in range(1, N_ETP // 2):
            total += recv_ref[ETP_PLACE[2 * y + c]].astype(F32)
        parts.append(total)
    first = iota((WID // 2, 128), 1) < 64
    top = jnp.where(first, parts[0][WID:], parts[1][WID:])
    bottom = jnp.where(first, pltpu.roll(parts[0][WID:], 64, 1), pltpu.roll(parts[1][WID:], 64, 1))
    whole = jnp.concatenate([parts[0][:WID], parts[1][:WID], jnp.concatenate([top, bottom], axis=0)], axis=1).astype(BF)
    src, rank = lane_slots()
    last = whole[128:]
    quarters = jnp.concatenate([jnp.where(rank % 4 == i, last, jnp.zeros_like(last)) for i in range(4)], axis=0)
    row = iota((GRID, SLOTS), 0)
    heads = (row == src * ROWS + rank).astype(BF)
    tails = (row == src * ROWS + CAP + rank // 4).astype(BF)
    out_ref[...] = (dot(heads, whole[:128], (1, 1)) + dot(tails, quarters, (1, 1))).astype(BF)


def unpack_kernel(slot_ref, recv_ref, out_ref):
    slot, row = slot_ref[...], iota((GRID, TOK), 0)
    rank = slot % ROWS
    heads = (row == slot).astype(BF)
    tails = (row == slot - rank + CAP + rank // 4).astype(BF)
    out_ref[:128, :] = dot(recv_ref[...], heads, (0, 0)).astype(BF)
    quarters = dot(recv_ref[...], tails, (0, 0))
    last = quarters[:32]
    for i in range(1, 4):
        last = jnp.where(rank % 4 == i, quarters[32 * i : 32 * (i + 1)], last)
    out_ref[128:, :] = last.astype(BF)


VM = pl.BlockSpec(memory_space=pltpu.VMEM)
SM = pl.BlockSpec(memory_space=pltpu.SMEM)
HBM = pl.BlockSpec(memory_space=pltpu.HBM)


def in_hbm(x):
    return pltpu.with_memory_space_constraint(x, pltpu.HBM)


def call(kernel, ins, outs, out_specs=VM, scratch=(), vmem=32 << 20, cost=None):
    return pl.pallas_call(
        kernel,
        out_shape=outs,
        in_specs=ins,
        out_specs=out_specs,
        scratch_shapes=list(scratch),
        cost_estimate=cost,
        compiler_params=pltpu.CompilerParams(vmem_limit_bytes=vmem),
    )


def expert_call(core, lo, hi, wg1, wu1, wd1, wg, wu, wd):
    shape = jax.ShapeDtypeStruct
    xt, g, score, columns, wd1 = call(
        prepare_kernel,
        [VM] * 2 + [HBM],
        [
            shape((256, D), BF),
            shape((D, 256), BF),
            shape((1, 256), F32),
            shape((WID, N_ETP), F32),
            pltpu.VMEM((HID, D), BF),
        ],
        [VM] * 5,
        [pltpu.VMEM((D, 256), BF), pltpu.SemaphoreType.DMA((2,))],
        vmem=16 << 20,
    )(lo, hi, in_hbm(wd1))
    return call(
        expert_kernel,
        [SM] + [VM] * 10,
        shape((N_ETP, WID * 3 // 2, 128), BF),
        vmem=20 << 20,
        cost=pl.CostEstimate(flops=10 * D * 512 * 256, bytes_accessed=12 << 20, transcendentals=512 * 256),
    )(core, xt, g, score, columns, wg1, wu1, wd1, wg, wu, wd)


def body(tokens, grad_out, expert_ids, router, gate_weight, up_weight, down_weight):
    me = lax.axis_index("ep").astype(jnp.int32).reshape(1)
    core = (lax.axis_index("etp") % 2).astype(jnp.int32).reshape(1)
    other = [(i, i ^ 1) for i in range(N_ETP)]
    own = [gate_weight[0], up_weight[0], down_weight[0]]
    shape = jax.ShapeDtypeStruct

    send, slot, line = call(
        pack_kernel,
        [SM] + [HBM] * 4,
        [shape((GRID, 2 * WID), BF), shape((1, TOK), jnp.int32), shape((8, SLOTS), F32)],
        [VM] * 3,
        [
            pltpu.VMEM((1, TOK), jnp.int32),
            pltpu.VMEM((WID, TOK), BF),
            pltpu.VMEM((WID, TOK), BF),
            pltpu.VMEM((EXPERTS, WID), BF),
            pltpu.SemaphoreType.DMA((4,)),
        ],
    )(me, *map(in_hbm, (expert_ids.reshape(1, TOK), tokens.T, grad_out.T, router.T)))
    recv = lax.all_to_all(send.reshape(EXPERTS, ROWS, 2 * WID), "ep", split_axis=0, concat_axis=0, tiled=True, axis_index_groups=[EP_ORDER])
    turned = call(turn_kernel, [VM, VM], shape((AG_ROWS, SLOTS), F32))(recv.reshape(GRID, 2 * WID), line)
    gathered = lax.all_gather(turned.astype(jnp.float16), "etp", axis=0, tiled=True).reshape(N_ETP, AG_ROWS, SLOTS)
    lo = lax.dynamic_slice(gathered, (0, 0, 128 * core[0]), (N_ETP, AG_ROWS, 128)).astype(BF)
    hi = gathered[:, :, 256:].astype(BF)
    wg, wu, wd = own
    wg1, wu1, wd1 = (lax.ppermute(w, "etp", other) for w in own)
    partial = expert_call(core, lo, hi, wg1, wu1, wd1, wg, wu, wd)
    parts = lax.all_to_all(partial, "etp", split_axis=0, concat_axis=0, tiled=True, axis_index_groups=[ETP_ORDER])
    summed = call(sum_kernel, [VM], shape((GRID, 128), BF))(parts)
    back = lax.all_to_all(summed.reshape(EXPERTS, ROWS, 128), "ep", split_axis=0, concat_axis=0, tiled=True, axis_index_groups=[EP_ORDER])
    out = call(unpack_kernel, [VM] * 2, shape((WID, TOK), BF))(slot, back.reshape(GRID, 128))
    return out.T


def solution(mesh):
    placed = (
        P("ep", "etp"),
        P("ep", "etp"),
        P("ep", None),
        P("etp", None),
        P("ep", None, "etp"),
        P("ep", None, "etp"),
        P("ep", "etp", None),
    )
    return jax.shard_map(body, mesh=mesh, in_specs=placed, out_specs=P("ep", "etp"), check_vma=False)
```

```python
import jax
import jax.numpy as jnp
from jax import lax
from jax.experimental import pallas as pl
from jax.experimental.pallas import tpu as pltpu
from jax.sharding import PartitionSpec as P

CAP = 12
ROWS = 16
EXPERTS = 32
TOK = 256
WID = 160
N_ETP = 16
D = WID * N_ETP
HID = 256
SLOTS = EXPERTS * CAP
HALF = SLOTS // 2
GRID = EXPERTS * ROWS
AG_ROWS = 2 * WID + 8
F32 = jnp.float32
BF = jnp.bfloat16


ETP_ORDER = [2 * y + y % 2 for y in range(8)] + [2 * y + 1 - y % 2 for y in range(8)]
ETP_PLACE = [ETP_ORDER.index(i) for i in range(N_ETP)]
EP_ORDER = [4 * z + (x + z) % 4 for x in range(4) for z in range(8)]


def ep_place(i):
    z = i // 4
    return (i - z) % 4 * 8 + z


def iota(shape, dim):
    return lax.broadcasted_iota(jnp.int32, shape, dim)


def dot(left, right, dims):
    return lax.dot_general(left, right, ((dims[:1], dims[1:]), ((), ())), preferred_element_type=F32)


def lane_slots():
    lane = iota((1, SLOTS), 1)
    half = jnp.where(lane < 256, lane // 128, lane // 64 % 2)
    at = jnp.where(lane < 256, lane % 128, 128 + lane % 64)
    return half * (EXPERTS // 2) + at // CAP, at % CAP


def slot_lanes():
    src, rank = lane_slots()
    return (iota((GRID, SLOTS), 0) == src * ROWS + rank).astype(BF)


def power(k):
    size, out = jnp.abs(k).astype(jnp.int32), jnp.ones_like(k)
    for bit in range(7):
        factor = jnp.where(k < 0, 2.0 ** -(1 << bit), 2.0 ** (1 << bit))
        out = jnp.where((size & (1 << bit)) != 0, out * factor, out)
    return out


def level(top):
    return 14.0 - jnp.clip(jnp.floor(jnp.log2(jnp.maximum(top, 1e-36))), -110.0, 14.0)


def pack_kernel(me_ref, ids_ref, x_ref, g_ref, router_ref, send_ref, slot_ref, line_ref, ids_v, x_v, g_v, router_v, sems):
    copies = [
        pltpu.make_async_copy(src, dst, sems.at[i])
        for i, (src, dst) in enumerate(((ids_ref, ids_v), (x_ref, x_v), (g_ref, g_v), (router_ref, router_v)))
    ]
    for c in copies:
        c.start()
    copies[0].wait()
    copies[3].wait()
    mine = (iota((8, EXPERTS), 1) == me_ref[0]).astype(BF)
    column = dot(mine, router_v[...], (1, 0))
    shift = level(jnp.max(jnp.abs(column), axis=1, keepdims=True))
    scaled = column * power(shift)
    row = jnp.concatenate([scaled[:, :128], scaled[:, :128], scaled[:, 128:], jnp.zeros((8, 96), F32)], axis=1)
    line_ref[...] = jnp.where(iota((8, SLOTS), 0) == 0, row, jnp.broadcast_to(shift, (8, SLOTS)))
    ids = ids_v[...]
    picked = iota((EXPERTS, TOK), 0) == ids
    before = (iota((TOK, TOK), 0) < iota((TOK, TOK), 1)).astype(BF)
    earlier = dot(picked.astype(BF), before, (1, 0))
    rank = jnp.sum(jnp.where(picked, earlier, 0.0), axis=0, keepdims=True).astype(jnp.int32)
    slot = ep_place(ids) * ROWS + rank
    slot_ref[...] = slot
    place = (iota((GRID, TOK), 0) == slot).astype(BF)
    copies[1].wait()
    copies[2].wait()
    both = jnp.concatenate([x_v[...], g_v[...]], axis=0)
    send_ref[...] = dot(place, both, (1, 1)).astype(BF)


def turn_kernel(recv_ref, router_ref, out_ref):
    both = dot(recv_ref[...], slot_lanes(), (0, 0))
    shifts = []
    for i in range(2):
        half = both[i * WID : (i + 1) * WID]
        shift = level(jnp.max(jnp.abs(half), axis=0, keepdims=True))
        out_ref[i * WID : (i + 1) * WID, :] = half * power(shift)
        shifts.append(shift)
    row = iota((8, SLOTS), 0)
    out_ref[2 * WID :, :] = jnp.where(row < 2, router_ref[...], jnp.where(row == 2, shifts[0], shifts[1]))


def prepare_kernel(lo_ref, hi_ref, wd_ref, xt_ref, g_ref, score_ref, router_ref, wd_out, x_ref, sems):
    size = HID // 2
    copies = []
    for p in range(2):
        at = pl.ds(p * size, size)
        copies.append(pltpu.make_async_copy(wd_ref.at[at], wd_out.at[at], sems.at[p]))
    for c in copies:
        c.start()

    def rows(first, count):
        return jnp.concatenate([lo_ref[:, first : first + count, :], hi_ref[:, first : first + count, :]], axis=2)

    extra = rows(2 * WID, 8).astype(F32)
    back = power(-extra)
    lines = jnp.concatenate([extra[j, :1] * back[j, 1:2] for j in range(N_ETP)], axis=0)[:, :WID]
    columns = lines.T
    router_ref[...] = columns
    logit = jnp.zeros((N_ETP, 256), F32)
    narrow = lines.astype(BF)
    for j in range(N_ETP):
        at = pl.ds(j * WID, WID)
        for first, ref, row in ((0, x_ref, 2), (WID, g_ref, 3)):
            scale = back[j, row : row + 1, :].astype(BF)
            ref[at, :128] = lo_ref[j, first : first + WID, :] * scale[:, :128]
            ref[at, 128:] = hi_ref[j, first : first + WID, :] * scale[:, 128:]
        logit += jnp.where(iota((N_ETP, 256), 0) == j, dot(narrow, x_ref[at, :], (1, 0)), 0.0)
    logit = jnp.sum(logit, axis=0, keepdims=True)
    score_ref[...] = 1.0 / (1.0 + jnp.exp(-logit))
    xt_ref[...] = x_ref[...].T
    for c in copies:
        c.wait()


def expert_kernel(core_ref, xt_ref, g_ref, score_ref, router_ref, wg0, wu0, wd0, wg1, wu1, wd1, out_ref):
    score, xt, g = score_ref[...], xt_ref[...], g_ref[...]
    d_gate, d_up = [], []
    d_score = jnp.zeros((1, 256), F32)
    for wg, wu, wd in ((wg0, wu0, wd0), (wg1, wu1, wd1)):
        gate = dot(xt, wg[...], (1, 0)).T
        up = dot(xt, wu[...], (1, 0)).T
        d_hidden = dot(wd[...], g, (1, 0))
        gate_pre, up_pre = gate * score, up * score
        sig = 1.0 / (1.0 + jnp.exp(-gate_pre))
        dg = (d_hidden * up_pre * (sig * (1.0 + gate_pre * (1.0 - sig)))).astype(BF)
        du = (d_hidden * (gate_pre * sig)).astype(BF)
        d_score += jnp.sum(dg.astype(F32) * gate + du.astype(F32) * up, axis=0, keepdims=True)
        d_gate.append(dg)
        d_up.append(du)
    d_logit = d_score * score * (1.0 - score)
    keep = (iota((WID // 2, 128), 1) // 64) == core_ref[0]
    for j in range(N_ETP):
        at = pl.ds(j * WID, WID)
        total = dot(wg0[at, :], d_gate[0], (1, 0)) + dot(wg1[at, :], d_gate[1], (1, 0))
        total += dot(wu0[at, :], d_up[0], (1, 0)) + dot(wu1[at, :], d_up[1], (1, 0))
        total = total * score + router_ref[:, j : j + 1] * d_logit
        out_ref[ETP_PLACE[j], :WID, :] = total[:, :128].astype(BF)
        top, bottom = total[: WID // 2, 128:], total[WID // 2 :, 128:]
        out_ref[ETP_PLACE[j], WID:, :] = jnp.where(keep, top, pltpu.roll(bottom, 64, 1)).astype(BF)


def sum_kernel(recv_ref, out_ref):
    parts = []
    for c in range(2):
        total = recv_ref[ETP_PLACE[c]].astype(F32)
        for y in range(1, N_ETP // 2):
            total += recv_ref[ETP_PLACE[2 * y + c]].astype(F32)
        parts.append(total)
    first = iota((WID // 2, 128), 1) < 64
    top = jnp.where(first, parts[0][WID:], parts[1][WID:])
    bottom = jnp.where(first, pltpu.roll(parts[0][WID:], 64, 1), pltpu.roll(parts[1][WID:], 64, 1))
    whole = jnp.concatenate([parts[0][:WID], parts[1][:WID], jnp.concatenate([top, bottom], axis=0)], axis=1).astype(BF)
    src, rank = lane_slots()
    last = whole[128:]
    quarters = jnp.concatenate([jnp.where(rank % 4 == i, last, jnp.zeros_like(last)) for i in range(4)], axis=0)
    row = iota((GRID, SLOTS), 0)
    heads = (row == src * ROWS + rank).astype(BF)
    tails = (row == src * ROWS + CAP + rank // 4).astype(BF)
    out_ref[...] = (dot(heads, whole[:128], (1, 1)) + dot(tails, quarters, (1, 1))).astype(BF)


def unpack_kernel(slot_ref, recv_ref, out_ref):
    slot, row = slot_ref[...], iota((GRID, TOK), 0)
    rank = slot % ROWS
    heads = (row == slot).astype(BF)
    tails = (row == slot - rank + CAP + rank // 4).astype(BF)
    both = dot(recv_ref[...], jnp.concatenate([heads, tails], axis=1), (0, 0))
    out_ref[:128, :] = both[:, :TOK].astype(BF)
    quarters = both[:, TOK:]
    last = quarters[:32]
    for i in range(1, 4):
        last = jnp.where(rank % 4 == i, quarters[32 * i : 32 * (i + 1)], last)
    out_ref[128:, :] = last.astype(BF)


VM = pl.BlockSpec(memory_space=pltpu.VMEM)
SM = pl.BlockSpec(memory_space=pltpu.SMEM)
HBM = pl.BlockSpec(memory_space=pltpu.HBM)


def in_hbm(x):
    return pltpu.with_memory_space_constraint(x, pltpu.HBM)


def call(kernel, ins, outs, out_specs=VM, scratch=(), vmem=32 << 20, cost=None):
    return pl.pallas_call(
        kernel,
        out_shape=outs,
        in_specs=ins,
        out_specs=out_specs,
        scratch_shapes=list(scratch),
        cost_estimate=cost,
        compiler_params=pltpu.CompilerParams(vmem_limit_bytes=vmem),
    )


def expert_call(core, lo, hi, wg1, wu1, wd1, wg, wu, wd):
    shape = jax.ShapeDtypeStruct
    xt, g, score, columns, wd1 = call(
        prepare_kernel,
        [VM] * 2 + [HBM],
        [
            shape((256, D), BF),
            shape((D, 256), BF),
            shape((1, 256), F32),
            shape((WID, N_ETP), F32),
            pltpu.VMEM((HID, D), BF),
        ],
        [VM] * 5,
        [pltpu.VMEM((D, 256), BF), pltpu.SemaphoreType.DMA((2,))],
        vmem=16 << 20,
    )(lo, hi, in_hbm(wd1))
    return call(
        expert_kernel,
        [SM] + [VM] * 10,
        shape((N_ETP, WID * 3 // 2, 128), BF),
        vmem=20 << 20,
        cost=pl.CostEstimate(flops=10 * D * 512 * 256, bytes_accessed=12 << 20, transcendentals=512 * 256),
    )(core, xt, g, score, columns, wg1, wu1, wd1, wg, wu, wd)


def body(tokens, grad_out, expert_ids, router, gate_weight, up_weight, down_weight):
    me = lax.axis_index("ep").astype(jnp.int32).reshape(1)
    core = (lax.axis_index("etp") % 2).astype(jnp.int32).reshape(1)
    other = [(i, i ^ 1) for i in range(N_ETP)]
    own = [gate_weight[0], up_weight[0], down_weight[0]]
    shape = jax.ShapeDtypeStruct

    send, slot, line = call(
        pack_kernel,
        [SM] + [HBM] * 4,
        [shape((GRID, 2 * WID), BF), shape((1, TOK), jnp.int32), shape((8, SLOTS), F32)],
        [VM] * 3,
        [
            pltpu.VMEM((1, TOK), jnp.int32),
            pltpu.VMEM((WID, TOK), BF),
            pltpu.VMEM((WID, TOK), BF),
            pltpu.VMEM((EXPERTS, WID), BF),
            pltpu.SemaphoreType.DMA((4,)),
        ],
    )(me, *map(in_hbm, (expert_ids.reshape(1, TOK), tokens.T, grad_out.T, router.T)))
    recv = lax.all_to_all(send.reshape(EXPERTS, ROWS, 2 * WID), "ep", split_axis=0, concat_axis=0, tiled=True, axis_index_groups=[EP_ORDER])
    turned = call(turn_kernel, [VM, VM], shape((AG_ROWS, SLOTS), F32))(recv.reshape(GRID, 2 * WID), line)
    gathered = lax.all_gather(turned.astype(jnp.float16), "etp", axis=0, tiled=True).reshape(N_ETP, AG_ROWS, SLOTS)
    lo = lax.dynamic_slice(gathered, (0, 0, 128 * core[0]), (N_ETP, AG_ROWS, 128)).astype(BF)
    hi = gathered[:, :, 256:].astype(BF)
    wg, wu, wd = own
    wg1, wu1, wd1 = (lax.ppermute(w, "etp", other) for w in own)
    partial = expert_call(core, lo, hi, wg1, wu1, wd1, wg, wu, wd)
    parts = lax.all_to_all(partial, "etp", split_axis=0, concat_axis=0, tiled=True, axis_index_groups=[ETP_ORDER])
    summed = call(sum_kernel, [VM], shape((GRID, 128), BF))(parts)
    back = lax.all_to_all(summed.reshape(EXPERTS, ROWS, 128), "ep", split_axis=0, concat_axis=0, tiled=True, axis_index_groups=[EP_ORDER])
    out = call(unpack_kernel, [VM] * 2, shape((WID, TOK), BF))(slot, back.reshape(GRID, 128))
    return out.T


def solution(mesh):
    placed = (
        P("ep", "etp"),
        P("ep", "etp"),
        P("ep", None),
        P("etp", None),
        P("ep", None, "etp"),
        P("ep", None, "etp"),
        P("ep", "etp", None),
    )
    return jax.shard_map(body, mesh=mesh, in_specs=placed, out_specs=P("ep", "etp"), check_vma=False)
```
